128 devices in a mesh: blk: 16 (over z, y_lo, core), grp: 8 (over x, y_hi).
Axes of the slice: x: 4, y: 4 (y_hi: 2, y_lo: 2; y = y_hi * 2 + y_lo), z: 4, core: 2. Of those that a mesh axis runs over, the one named last changes fastest.
Arguments:
- tgt_pos: float32 [3, 524288], P(None, ('blk', 'grp')), may hold values from -6 to 6
- tgt_area: float32 [524288], P(('blk', 'grp')), may hold values from 0.5 to 2
- tgt_cond: int32 [524288], P(('blk', 'grp')), may hold values from 0 to 63
- adjoint: float32 [64, 524288], P(None, ('blk', 'grp')), may hold values from -6 to 6
- src_pos: float32 [3, 8192], P(None, 'blk'), may hold values from -6 to 6
- src_nrm: float32 [3, 8192], P(None, 'blk'), may hold values from -6 to 6
- src_area: float32 [8192], P('blk'), may hold values from 0.005 to 0.05
- density: float32 [64, 8192], P(None, 'blk'), may hold values from -6 to 6
- cond_scale: float32 [64], replicated, may hold values from 0.5 to 4
- near_tgt: int32 [524288], P(('blk', 'grp')), may hold values from 0 to 524287, as said below
- near_src: int32 [524288], P(('blk', 'grp')), may hold values from 0 to 8191
- near_coef: float32 [524288], P(('blk', 'grp')), may hold values from 0.02 to 0.2
Outputs:
- tgt_grad: float32 [3, 524288], P(None, ('blk', 'grp'))
- src_grad: float32 [3, 8192], P(None, ('blk', 'grp'))
The draws below stay inside these ranges and needn't reach their ends.
Inputs may be any that keep to these rules, and one draw needn't show every extreme that they name: Entry p of near_tgt lies among the targets k * 4096 to (k + 1) * 4096 - 1 with k = p // 4096.
All inputs are finite; a program needn't handle non-finite values.
Results may differ from the reference program's by a relative error of at most 0.0003.
Values sent between devices are 32-bit elements; how exact they have to be, the bound alone decides.
A program may use at most 768 MiB of HBM per device.

```python
import math
import jax
import jax.numpy as jnp
from jax import lax

EXC = 64
TGT_DEV = 4096
NEAR_DEV = 4096
TGT = 524288
SRC = 8192
NEAR = 524288


def draw_near_tgt(key, part):
    key = jax.random.fold_in(key, 11)
    index = jnp.arange(NEAR, dtype=jnp.int32)
    owner = index // NEAR_DEV
    slot = index % NEAR_DEV
    offset = jax.random.randint(key, (NEAR,), 0, TGT_DEV, dtype=jnp.int32)
    offset = jnp.where(slot == 0, 0, jnp.where(slot == NEAR_DEV - 1, TGT_DEV - 1, offset))
    return (owner * TGT_DEV + offset).astype(jnp.int32)


def draw_near_src(key, part):
    key = jax.random.fold_in(key, 23)
    index = jnp.arange(NEAR, dtype=jnp.int32)
    value = jax.random.randint(key, (NEAR,), 0, SRC, dtype=jnp.int32)
    value = jnp.where(index == 0, 0, jnp.where(index == NEAR - 1, SRC - 1, value))
    return value.astype(jnp.int32)


def plant(result, key, low, high):
    spot = [jax.random.randint(jax.random.fold_in(key, axis), (), 0, length) for axis, length in enumerate(result.shape)]
    main_axis = result.shape.index(max(result.shape))
    beside = spot[:main_axis] + [(spot[main_axis] + 1) % result.shape[main_axis]] + spot[main_axis + 1:]
    return result.at[tuple(spot)].set(low).at[tuple(beside)].set(high)


def shard_levels(own_key, extent, shards, smallest, high):
    def one(position, blocks):
        heights = jax.random.uniform(jax.random.fold_in(jax.random.fold_in(own_key, 6), position), (blocks,), jnp.float32, smallest / len(shards), high / len(shards))
        return jnp.repeat(jnp.exp(heights), extent[position] // blocks).reshape((-1,) + (1,) * (len(extent) - position - 1))

    level = one(*shards[0])
    for cut in shards[1:]:
        level = level * one(*cut)
    return level


def noise(key, extent, spread, most, shards=(), held_as=jnp.bfloat16):
    drawn = spread * jax.random.normal(key, extent, jnp.float32)
    if shards:
        drawn = drawn * shard_levels(key, extent, shards, -0.22, 0.18)
    return jnp.clip(drawn, -most, most).astype(held_as)


def setup_inputs(seed: int = 0) -> dict:
    splits = jax.random.split(jax.random.key(seed), 13)
    tgt_pos = noise(splits[0], (3, TGT), 1.0, 6.0, ((1, 128),), jnp.float32)
    tgt_area = jnp.clip(jnp.exp(math.log(2.0) - 1.3862944 * jax.random.uniform(splits[1], (TGT,), jnp.float32) ** shard_levels(splits[1], (TGT,), ((0, 128),), -0.2, 0.2)), 0.5, 2.0)
    tgt_cond = plant(jax.random.randint(splits[2], (TGT,), 0, EXC), jax.random.fold_in(splits[2], 1), 0, EXC - 1).astype(jnp.int32)
    adjoint = noise(splits[3], (EXC, TGT), 1.0, 6.0, ((1, 128),), jnp.float32)
    src_pos = noise(splits[4], (3, SRC), 1.0, 6.0, ((1, 16),), jnp.float32)
    src_nrm = noise(splits[5], (3, SRC), 1.0, 6.0, ((1, 16),), jnp.float32)
    src_area = jnp.clip(jnp.exp(math.log(0.05) - 2.3025851 * jax.random.uniform(splits[6], (SRC,), jnp.float32) ** shard_levels(splits[6], (SRC,), ((0, 16),), -0.2, 0.2)), 0.005, 0.05)
    density = noise(splits[7], (EXC, SRC), 1.0, 6.0, ((1, 16),), jnp.float32)
    cond_scale = jnp.clip(jnp.exp(jax.random.uniform(splits[8], (EXC,), jnp.float32, math.log(0.5), math.log(4.0))), 0.5, 4.0)
    near_tgt = draw_near_tgt(jax.random.fold_in(splits[12], 71), 0)
    near_src = draw_near_src(jax.random.fold_in(splits[12], 71), 0)
    near_coef = jnp.clip(jnp.exp(math.log(0.2) - 2.3025851 * jax.random.uniform(splits[11], (NEAR,), jnp.float32) ** shard_levels(splits[11], (NEAR,), ((0, 128),), -0.2, 0.2)), 0.02, 0.2)
    return dict(tgt_pos=tgt_pos, tgt_area=tgt_area, tgt_cond=tgt_cond, adjoint=adjoint, src_pos=src_pos, src_nrm=src_nrm, src_area=src_area, density=density, cond_scale=cond_scale, near_tgt=near_tgt, near_src=near_src, near_coef=near_coef)


SOFTEN = 0.05
INV_FOUR_PI = 1.0 / (4.0 * math.pi)

def far_terms(pos, weight, adj, src_pos, src_nrm, src_area, density):
    coupling = lax.dot_general(adj, density, (((0,), (0,)), ((), ())), precision=lax.Precision.HIGHEST)
    scale = weight[:, None] * src_area[None, :] * coupling * INV_FOUR_PI
    dx = pos[0][:, None] - src_pos[0][None, :]
    dy = pos[1][:, None] - src_pos[1][None, :]
    dz = pos[2][:, None] - src_pos[2][None, :]
    r2 = dx * dx + dy * dy + dz * dz + SOFTEN
    inv = lax.rsqrt(r2)
    inv3 = inv * inv * inv
    ndot = src_nrm[0][None, :] * dx + src_nrm[1][None, :] * dy + src_nrm[2][None, :] * dz
    radial = 3.0 * ndot * inv3 * inv * inv
    gx = (src_nrm[0][None, :] * inv3 - radial * dx) * scale
    gy = (src_nrm[1][None, :] * inv3 - radial * dy) * scale
    gz = (src_nrm[2][None, :] * inv3 - radial * dz) * scale
    grad_t = jnp.stack([lax.optimization_barrier(jnp.sum(gx, 1)), lax.optimization_barrier(jnp.sum(gy, 1)), lax.optimization_barrier(jnp.sum(gz, 1))])
    grad_s = -jnp.stack([lax.optimization_barrier(jnp.sum(gx, 0)), lax.optimization_barrier(jnp.sum(gy, 0)), lax.optimization_barrier(jnp.sum(gz, 0))])
    return (grad_t, grad_s)

def reference(tgt_pos, tgt_area, tgt_cond, adjoint, src_pos, src_nrm, src_area, density, cond_scale, near_tgt, near_src, near_coef):
    weight_t = tgt_area * cond_scale[tgt_cond]
    tiles = TGT // TGT_DEV

    def tile(carry, index):
        start = (index * TGT_DEV).astype(jnp.int32)
        pos = lax.dynamic_slice_in_dim(tgt_pos, start, TGT_DEV, 1)
        weight = lax.dynamic_slice_in_dim(weight_t, start, TGT_DEV, 0)
        adj = lax.dynamic_slice_in_dim(adjoint, start, TGT_DEV, 1)
        grad_t, grad_s = far_terms(pos, weight, adj, src_pos, src_nrm, src_area, density)
        return (carry + grad_s, grad_t)
    src_grad, parts = lax.scan(tile, jnp.zeros((3, SRC), jnp.float32), jnp.arange(tiles, dtype=jnp.int32))
    tgt_grad = jnp.transpose(parts, (1, 0, 2)).reshape(3, TGT)
    pair_adj = adjoint[:, near_tgt]
    pair_den = density[:, near_src]
    coupled = lax.optimization_barrier(jnp.sum(pair_adj * pair_den, axis=0)) * near_coef * weight_t[near_tgt]
    near_val = coupled[None, :] * src_nrm[:, near_src]
    tgt_grad = tgt_grad.at[:, near_tgt].add(near_val)
    src_grad = src_grad.at[:, near_src].add(-near_val)
    return (tgt_grad, src_grad)
```

```python
import functools
import math

import jax
import jax.numpy as jnp
from jax import lax
from jax.experimental import pallas as pl
from jax.experimental.pallas import tpu as pltpu
from jax.sharding import PartitionSpec as P

SOFTEN = 0.05
INV_FOUR_PI = 1.0 / (4.0 * math.pi)
MESH = pl.DeviceIdType.MESH
F32 = jnp.float32
BF16 = jnp.bfloat16
LANES = 128
WIDTH = 64
PACK = 72
BLOCK = 256
CHUNK = 512
SUM_ROWS = 16


def part(x):
    return x.astype(BF16).astype(F32)


def three_parts(x):
    first = part(x)
    second = part(x - first)
    return first, second, part(x - first - second)


def grid_parts(x):
    first = jnp.floor(x * 16.0 + 0.5) * 0.0625
    rest = x - first
    second = part(rest)
    return first, second, part(rest - second), rest


def square_parts(first, rest):
    square = jnp.sum(first * first, axis=0, keepdims=True)
    whole = jnp.floor(square)
    left = jnp.sum((2.0 * first + rest) * rest, axis=0, keepdims=True)
    return whole, square - whole, left


def rows(pieces, total):
    count = sum(p.shape[0] for p in pieces)
    width = pieces[0].shape[1]
    if count < total:
        pieces = list(pieces) + [jnp.zeros((total - count, width), F32)]
    return jnp.concatenate(pieces, axis=0)


def target_features(pos):
    t1, t2, t3, rest = grid_parts(pos)
    whole, fraction, left = square_parts(t1, rest)
    ones = jnp.ones((5, pos.shape[1]), F32)
    return rows([ones, t1, whole, fraction, t1, t1, t2, t2, t2, t3, t3, *three_parts(left)], WIDTH)


def source_features(pos, nrm):
    s1, s2, s3, rest = grid_parts(pos)
    whole, fraction, left = square_parts(s1, rest)
    zero = jnp.zeros((1, pos.shape[1]), F32)
    one = jnp.ones((1, pos.shape[1]), F32)
    radius = rows(
        [whole, fraction, *three_parts(left + SOFTEN)]
        + [-2.0 * s1, one, one, -2.0 * s2, -2.0 * s3, -2.0 * s1, -2.0 * s2, -2.0 * s3, -2.0 * s1, -2.0 * s2]
        + [one, one, one],
        WIDTH,
    )
    triple = 3.0 * nrm
    n1, n2, n3 = three_parts(triple)
    offset = -jnp.sum(triple * pos, axis=0, keepdims=True)
    normal = rows(
        [*three_parts(offset), zero, zero]
        + [n1, zero, zero, n2, n3, n1, n2, n3, n1, n2]
        + [zero, zero, zero],
        WIDTH,
    )
    return radius, normal


def pair_kernel(
    near_tgt, near_src, tgt_pos, tgt_area, tgt_cond, adjoint, cond_scale, near_tgt_row, near_src_row, near_coef, packs,
    tgt_out, src_out,
    held, left_m, rhs_c, rhs_g, src_rows, src_table, spread, tgt_sum, src_sum, product, buf0, buf1,
):
    tgt_count = tgt_pos.shape[1]
    parts, _, per = packs.shape
    total = parts * per
    halves = per // BLOCK
    blocks = total // BLOCK
    chunks = tgt_count // CHUNK

    def target_prep(i, _):
        cols = pl.ds(pl.multiple_of(i * CHUNK, CHUNK), CHUNK)
        cond = tgt_cond[:, cols]
        hit = lax.broadcasted_iota(jnp.int32, (WIDTH, CHUNK), 0) == cond
        weight = tgt_area[:, cols] * jnp.sum(jnp.where(hit, cond_scale[...], 0.0), axis=0, keepdims=True)
        stacked = jnp.concatenate([adjoint[:, cols] * weight, target_features(tgt_pos[:, cols])], axis=0)
        flat = jnp.transpose(stacked)
        held[cols, :] = flat
        high = part(flat)
        low = flat - high
        lane = lax.broadcasted_iota(jnp.int32, (CHUNK, LANES), 1)
        second = jnp.where(lane >= WIDTH, pltpu.roll(high, WIDTH, 1), low)
        left_m[cols, 0:LANES] = high.astype(BF16)
        left_m[cols, LANES : 2 * LANES] = second.astype(BF16)
        return 0

    lax.fori_loop(0, chunks, target_prep, 0)

    feature = lax.broadcasted_iota(jnp.int32, (LANES, 3 * LANES), 0) - WIDTH
    which = lax.broadcasted_iota(jnp.int32, (LANES, 3 * LANES), 1) // LANES
    pick = (feature == 5 + which) | (feature == 16 + which) | (feature == 25 + which)
    picker = pick.astype(F32).astype(BF16)

    def spread_prep(i, _):
        cols = pl.ds(pl.multiple_of(i * CHUNK, CHUNK), CHUNK)
        spread[cols, :] = jnp.dot(left_m[cols, 0:LANES], picker, preferred_element_type=F32)
        tgt_sum[cols, :] = jnp.zeros((CHUNK, 3 * LANES), F32)
        return 0

    lax.fori_loop(0, chunks, spread_prep, 0)

    zeros = jnp.zeros((WIDTH, BLOCK), BF16)

    def source_prep(b, _):
        for h in range(halves):
            pack = packs[b, :, h * BLOCK : (h + 1) * BLOCK]
            block = b * halves + h
            density = pack[0:WIDTH]
            pos = pack[WIDTH : WIDTH + 3]
            nrm = pack[WIDTH + 3 : WIDTH + 6]
            scaled = density * (pack[WIDTH + 6 : WIDTH + 7] * INV_FOUR_PI)
            high = scaled.astype(BF16)
            low = (scaled - high.astype(F32)).astype(BF16)
            rhs_c[block, 0:WIDTH, :] = high
            rhs_c[block, WIDTH : 2 * WIDTH, :] = zeros
            rhs_c[block, 2 * WIDTH : 3 * WIDTH, :] = high
            rhs_c[block, 3 * WIDTH : 4 * WIDTH, :] = low
            radius, normal = source_features(pos, nrm)
            rhs_g[block, 0:WIDTH, 0:BLOCK] = zeros
            rhs_g[block, 0:WIDTH, BLOCK : 2 * BLOCK] = zeros
            rhs_g[block, WIDTH : 2 * WIDTH, 0:BLOCK] = radius.astype(BF16)
            rhs_g[block, WIDTH : 2 * WIDTH, BLOCK : 2 * BLOCK] = normal.astype(BF16)
            src_rows[block] = pack[WIDTH : WIDTH + 8]
            src_sum[block] = jnp.zeros((24, BLOCK), F32)
            stacked = jnp.concatenate([density, rows([nrm], WIDTH)], axis=0)
            src_table[pl.ds(pl.multiple_of(block * BLOCK, BLOCK), BLOCK), :] = jnp.transpose(stacked)
        return 0

    lax.fori_loop(0, parts, source_prep, 0)

    steps = blocks * chunks

    def products(k, buf):
        b, i = k // chunks, lax.rem(k, chunks)
        rows_at = pl.ds(pl.multiple_of(i * CHUNK, CHUNK), CHUNK)
        buf[:, 0:BLOCK] = jnp.dot(left_m[rows_at, :], rhs_c[b], preferred_element_type=F32)
        buf[:, BLOCK : 3 * BLOCK] = jnp.dot(left_m[rows_at, 0:LANES], rhs_g[b], preferred_element_type=F32)

    def sums(k, buf):
        b, i = k // chunks, lax.rem(k, chunks)
        base = i * CHUNK
        src = src_rows[b]
        wide = BLOCK // LANES
        lane = [slice(j * LANES, (j + 1) * LANES) for j in range(wide)]
        row = [[jnp.broadcast_to(src[q : q + 1, lane[j]], (8, LANES)) for q in range(6)] for j in range(wide)]
        acc = [[src_sum[b, 8 * c : 8 * c + 8, lane[j]] for c in range(3)] for j in range(wide)]
        for r in range(CHUNK // 8):
            at = pl.ds(pl.multiple_of(base + 8 * r, 8), 8)
            here = [spread[at, c * LANES : (c + 1) * LANES] for c in range(3)]
            total_t = [None] * 3
            for j in range(wide):
                coupling = buf[8 * r : 8 * r + 8, j * LANES : (j + 1) * LANES]
                radius = buf[8 * r : 8 * r + 8, BLOCK + j * LANES : BLOCK + (j + 1) * LANES]
                normal = buf[8 * r : 8 * r + 8, 2 * BLOCK + j * LANES : 2 * BLOCK + (j + 1) * LANES]
                inv = lax.rsqrt(radius)
                inv2 = inv * inv
                scale = (coupling * inv) * inv2
                along = normal * inv2
                for c in range(3):
                    g = scale * (row[j][3 + c] - along * (here[c] - row[j][c]))
                    acc[j][c] = acc[j][c] + g
                    total_t[c] = g if total_t[c] is None else total_t[c] + g
            for c in range(3):
                tgt_sum[at, c * LANES : (c + 1) * LANES] += total_t[c]
        for j in range(wide):
            for c in range(3):
                src_sum[b, 8 * c : 8 * c + 8, lane[j]] = acc[j][c]

    products(0, buf0)

    def far(h, _):
        k = 2 * h
        products(k + 1, buf1)
        sums(k, buf0)
        products(jnp.minimum(k + 2, steps - 1), buf0)
        sums(k + 1, buf1)
        return 0

    lax.fori_loop(0, steps // 2, far, 0)

    pairs = near_coef.shape[1]
    first_target = (near_tgt[0] // tgt_count) * tgt_count

    def gather(i, _):
        for u in range(16):
            p = i * 16 + u
            t = near_tgt[p] - first_target
            product[pl.ds(p, 1), :] = held[pl.ds(t, 1), :] * src_table[pl.ds(near_src[p], 1), :]
        return 0

    lax.fori_loop(0, pairs // 16, gather, 0)

    flat = jnp.transpose(product[...])
    coupled = jnp.sum(flat[0:WIDTH], axis=0, keepdims=True) * near_coef[...]
    value = coupled * flat[WIDTH : WIDTH + 3]
    high = part(value)
    both = rows([high, part(value - high)], 8)

    def scatter(index, groups):
        row_at, lane_at = index // LANES, lax.rem(index, LANES)
        chosen = [jnp.where(row_at == g, both, 0.0).astype(BF16) for g in range(groups)]
        lanes = (lax.broadcasted_iota(jnp.int32, (LANES, pairs), 0) == lane_at).astype(F32).astype(BF16)
        return lax.dot_general(
            jnp.concatenate(chosen, axis=0), lanes, (((1,), (1,)), ((), ())), preferred_element_type=F32
        )

    local = near_tgt_row[...] - first_target
    to_tgt = scatter(local, tgt_count // LANES)
    to_src = scatter(near_src_row[...], total // LANES)

    lane = lax.broadcasted_iota(jnp.int32, (LANES, LANES), 1)
    for g in range(tgt_count // LANES):
        at = slice(g * LANES, (g + 1) * LANES)
        merged = jnp.zeros((LANES, LANES), F32)
        for c in range(3):
            one = jnp.sum(tgt_sum[at, c * LANES : (c + 1) * LANES], axis=1, keepdims=True)
            merged = jnp.where(lane == c, one, merged)
        near = to_tgt[8 * g : 8 * g + 8]
        tgt_out[:, at] = jnp.transpose(merged)[0:3] + near[0:3] + near[3:6]
    quarters = per // LANES
    for b in range(parts):
        src_out[b, 3 * quarters :, :] = jnp.zeros((src_out.shape[1] - 3 * quarters, LANES), F32)
        for q in range(quarters):
            g = b * quarters + q
            block, j = divmod(g, BLOCK // LANES)
            near = to_src[8 * g : 8 * g + 8]
            near = near[0:3] + near[3:6]
            at = slice(j * LANES, (j + 1) * LANES)
            for c in range(3):
                far_sum = jnp.sum(src_sum[block, 8 * c : 8 * c + 8, at], axis=0, keepdims=True)
                row = c * quarters + q
                src_out[b, row : row + 1, :] = -far_sum - near[c : c + 1]


def pair_sums(tgt_pos, tgt_area, tgt_cond, adjoint, cond_scale, near_tgt, near_src, near_coef, packs):
    tgt_count = tgt_pos.shape[1]
    pairs = near_coef.shape[0]
    parts, _, per = packs.shape
    total = parts * per
    blocks = total // BLOCK
    vmem = pl.BlockSpec(memory_space=pltpu.VMEM)
    smem = pl.BlockSpec(memory_space=pltpu.SMEM)
    return pl.pallas_call(
        pair_kernel,
        out_shape=[jax.ShapeDtypeStruct((3, tgt_count), F32), jax.ShapeDtypeStruct((parts, SUM_ROWS, LANES), F32)],
        in_specs=[smem, smem] + [vmem] * 9,
        out_specs=[vmem, vmem],
        scratch_shapes=[
            pltpu.VMEM((tgt_count, LANES), F32),
            pltpu.VMEM((tgt_count, 2 * LANES), BF16),
            pltpu.VMEM((blocks, 4 * WIDTH, BLOCK), BF16),
            pltpu.VMEM((blocks, 2 * WIDTH, 2 * BLOCK), BF16),
            pltpu.VMEM((blocks, 8, BLOCK), F32),
            pltpu.VMEM((total, LANES), F32),
            pltpu.VMEM((tgt_count, 3 * LANES), F32),
            pltpu.VMEM((tgt_count, 3 * LANES), F32),
            pltpu.VMEM((blocks, 24, BLOCK), F32),
            pltpu.VMEM((pairs, LANES), F32),
            pltpu.VMEM((CHUNK, 3 * BLOCK), F32),
            pltpu.VMEM((CHUNK, 3 * BLOCK), F32),
        ],
        compiler_params=pltpu.CompilerParams(vmem_limit_bytes=60 * 2**20),
    )(
        near_tgt, near_src, tgt_pos, tgt_area[None, :], tgt_cond[None, :], adjoint, cond_scale[:, None],
        near_tgt[None, :], near_src[None, :], near_coef[None, :], packs,
    )


def greet(peers):
    barrier = pltpu.get_barrier_semaphore()
    for peer in peers:
        pl.semaphore_signal(barrier, inc=1, device_id=peer, device_id_type=MESH)
    pl.semaphore_wait(barrier, len(peers))


def gather_kernel(n, own, out, send_sem, recv_sem, local_sem):
    me = lax.axis_index("blk")
    others = [lax.rem(me + k, n) for k in range(1, n)]
    greet([{"blk": other} for other in others])
    copies = []
    for k, other in enumerate(others):
        copy = pltpu.make_async_remote_copy(
            src_ref=own, dst_ref=out.at[me], send_sem=send_sem.at[k], recv_sem=recv_sem.at[k],
            device_id={"blk": other}, device_id_type=MESH,
        )
        copy.start()
        copies.append(copy)
    mine = pltpu.make_async_copy(own, out.at[me], local_sem)
    mine.start()
    mine.wait()
    for copy in copies:
        copy.wait()


def gather_sources(pack, n):
    hbm = pl.BlockSpec(memory_space=pl.ANY)
    return pl.pallas_call(
        functools.partial(gather_kernel, n),
        out_shape=jax.ShapeDtypeStruct((n,) + pack.shape, F32),
        in_specs=[hbm],
        out_specs=hbm,
        scratch_shapes=[
            pltpu.SemaphoreType.DMA((n - 1,)),
            pltpu.SemaphoreType.DMA((n - 1,)),
            pltpu.SemaphoreType.DMA,
        ],
        compiler_params=pltpu.CompilerParams(collective_id=0, has_side_effects=True),
    )(pack)


def reduce_kernel(n, groups, sums, out, first, second, mine, send1, recv1, send2, recv2):
    me, grp = lax.axis_index("blk"), lax.axis_index("grp")
    blk_others = [lax.rem(me + k, n) for k in range(1, n)]
    grp_others = [lax.rem(grp + k, groups) for k in range(1, groups)]
    greet([{"blk": other} for other in blk_others] + [{"grp": other} for other in grp_others])
    copies = []
    for k, other in enumerate(blk_others):
        copy = pltpu.make_async_remote_copy(
            src_ref=sums.at[other], dst_ref=first.at[k], send_sem=send1.at[k], recv_sem=recv1.at[k],
            device_id={"blk": other}, device_id_type=MESH,
        )
        copy.start()
        copies.append(copy)
    total = sums[me]
    for k, copy in enumerate(copies):
        copy.wait_recv()
        total = total + first[k]
    quarters = groups // 2
    for q in range(quarters):
        mine[q] = jnp.concatenate(
            [total[c * quarters + q : c * quarters + q + 1] for c in range(3)] + [jnp.zeros((5, LANES), F32)], axis=0
        )
    more = []
    for k, other in enumerate(grp_others):
        copy = pltpu.make_async_remote_copy(
            src_ref=mine.at[other // 2], dst_ref=second.at[k], send_sem=send2.at[k], recv_sem=recv2.at[k],
            device_id={"grp": other}, device_id_type=MESH,
        )
        copy.start()
        more.append(copy)
    result = mine[grp // 2]
    for k, copy in enumerate(more):
        copy.wait_recv()
        result = result + second[k]
    half = LANES // 2
    out[...] = jnp.where(lax.rem(grp, 2) == 1, result[0:3, half:], result[0:3, 0:half])
    for copy in copies + more:
        copy.wait_send()


def reduce_sources(sums, n, groups):
    vmem = pl.BlockSpec(memory_space=pltpu.VMEM)
    return pl.pallas_call(
        functools.partial(reduce_kernel, n, groups),
        out_shape=jax.ShapeDtypeStruct((3, LANES // 2), F32),
        in_specs=[vmem],
        out_specs=vmem,
        scratch_shapes=[
            pltpu.VMEM((n - 1, SUM_ROWS, LANES), F32),
            pltpu.VMEM((groups - 1, 8, LANES), F32),
            pltpu.VMEM((groups // 2, 8, LANES), F32),
            pltpu.SemaphoreType.DMA((n - 1,)),
            pltpu.SemaphoreType.DMA((n - 1,)),
            pltpu.SemaphoreType.DMA((groups - 1,)),
            pltpu.SemaphoreType.DMA((groups - 1,)),
        ],
        compiler_params=pltpu.CompilerParams(collective_id=1, has_side_effects=True),
    )(sums)


def per_device(
    tgt_pos, tgt_area, tgt_cond, adjoint, src_pos, src_nrm, src_area, density, cond_scale, near_tgt, near_src, near_coef
):
    n, groups = lax.axis_size("blk"), lax.axis_size("grp")
    filler = jnp.zeros((PACK - WIDTH - 7, src_pos.shape[1]), F32)
    pack = jnp.concatenate([density, src_pos, src_nrm, src_area[None, :], filler], axis=0)
    packs = gather_sources(pack, n)
    tgt_grad, sums = pair_sums(
        tgt_pos, tgt_area, tgt_cond, adjoint, cond_scale, near_tgt, near_src, near_coef, packs
    )
    return tgt_grad, reduce_sources(sums, n, groups)


def solution(mesh):
    placed = (
        P(None, ("blk", "grp")),
        P(("blk", "grp")),
        P(("blk", "grp")),
        P(None, ("blk", "grp")),
        P(None, "blk"),
        P(None, "blk"),
        P("blk"),
        P(None, "blk"),
        P(),
        P(("blk", "grp")),
        P(("blk", "grp")),
        P(("blk", "grp")),
    )
    return jax.shard_map(
        per_device,
        mesh=mesh,
        in_specs=placed,
        out_specs=(P(None, ("blk", "grp")), P(None, ("blk", "grp"))),
        check_vma=False,
    )
```

```python
import functools
import math

import jax
import jax.numpy as jnp
from jax import lax
from jax.experimental import pallas as pl
from jax.experimental.pallas import tpu as pltpu
from jax.sharding import PartitionSpec as P

SOFTEN = 0.05
INV_FOUR_PI = 1.0 / (4.0 * math.pi)
MESH = pl.DeviceIdType.MESH
F32 = jnp.float32
BF16 = jnp.bfloat16
LANES = 128
WIDTH = 64
PACK = 72
BLOCK = 256
CHUNK = 512
PIECE = 32
GROUP = 16
SUM_ROWS = 16


def part(x):
    return x.astype(BF16).astype(F32)


def three_parts(x):
    first = part(x)
    second = part(x - first)
    return first, second, part(x - first - second)


def grid_parts(x):
    first = jnp.floor(x * 16.0 + 0.5) * 0.0625
    rest = x - first
    second = part(rest)
    return first, second, part(rest - second), rest


def square_parts(first, rest):
    square = jnp.sum(first * first, axis=0, keepdims=True)
    whole = jnp.floor(square)
    left = jnp.sum((2.0 * first + rest) * rest, axis=0, keepdims=True)
    return whole, square - whole, left


def rows(pieces, total):
    count = sum(p.shape[0] for p in pieces)
    width = pieces[0].shape[1]
    if count < total:
        pieces = list(pieces) + [jnp.zeros((total - count, width), F32)]
    return jnp.concatenate(pieces, axis=0)


def target_features(pos):
    t1, t2, t3, rest = grid_parts(pos)
    whole, fraction, left = square_parts(t1, rest)
    ones = jnp.ones((5, pos.shape[1]), F32)
    return rows([ones, t1, whole, fraction, t1, t1, t2, t2, t2, t3, t3, *three_parts(left)], WIDTH)


def source_features(pos, nrm):
    s1, s2, s3, rest = grid_parts(pos)
    whole, fraction, left = square_parts(s1, rest)
    zero = jnp.zeros((1, pos.shape[1]), F32)
    one = jnp.ones((1, pos.shape[1]), F32)
    radius = rows(
        [whole, fraction, *three_parts(left + SOFTEN)]
        + [-2.0 * s1, one, one, -2.0 * s2, -2.0 * s3, -2.0 * s1, -2.0 * s2, -2.0 * s3, -2.0 * s1, -2.0 * s2]
        + [one, one, one],
        WIDTH,
    )
    triple = 3.0 * nrm
    n1, n2, n3 = three_parts(triple)
    offset = -jnp.sum(triple * pos, axis=0, keepdims=True)
    normal = rows(
        [*three_parts(offset), zero, zero]
        + [n1, zero, zero, n2, n3, n1, n2, n3, n1, n2]
        + [zero, zero, zero],
        WIDTH,
    )
    return radius, normal


def pair_kernel(*refs):
    pieces = CHUNK // PIECE
    units = [pltpu.ACC(unit)((PIECE, BLOCK), F32) for unit in range(2) for _ in range(pieces + pieces // 2)]
    pl.run_scoped(lambda *accs: pair_body(accs, *refs), *units)


def pair_body(
    accs,
    near_tgt, near_src, tgt_pos, tgt_area, tgt_cond, adjoint, cond_scale, near_tgt_row, near_src_row, near_coef, packs,
    tgt_out, src_out,
    held, left_m, right_m, src_rows, src_table, spread, tgt_sum, src_sum, product, buf0, buf1,
):
    tgt_count = tgt_pos.shape[1]
    parts, _, per = packs.shape
    total = parts * per
    halves = per // BLOCK
    blocks = total // BLOCK
    chunks = tgt_count // CHUNK
    pairs = near_coef.shape[1]
    first_target = (near_tgt[0] // tgt_count) * tgt_count

    scales = jnp.transpose(jnp.broadcast_to(cond_scale[...], (LANES, LANES)))[0:WIDTH]
    scales = jnp.concatenate([scales] * (CHUNK // LANES), axis=1)

    def target_prep(i, _):
        cols = pl.ds(pl.multiple_of(i * CHUNK, CHUNK), CHUNK)
        hit = lax.broadcasted_iota(jnp.int32, (WIDTH, CHUNK), 0) == tgt_cond[:, cols]
        weight = tgt_area[:, cols] * jnp.sum(jnp.where(hit, scales, 0.0), axis=0, keepdims=True)
        stacked = jnp.concatenate([adjoint[:, cols] * weight, target_features(tgt_pos[:, cols])], axis=0)
        flat = jnp.transpose(stacked)
        held[cols, :] = flat
        high = part(flat)
        low = flat - high
        lane = lax.broadcasted_iota(jnp.int32, (CHUNK, LANES), 1)
        second = jnp.where(lane >= WIDTH, pltpu.roll(high, WIDTH, 1), low)
        left_m[cols, 0:LANES] = high.astype(BF16)
        left_m[cols, LANES : 2 * LANES] = second.astype(BF16)
        return 0

    lax.fori_loop(0, chunks, target_prep, 0)

    count = CHUNK // PIECE
    half = count // 2
    radius_acc, first_acc = accs[0:count], accs[count : count + half]
    coupling_acc, second_acc = accs[count + half : 2 * count + half], accs[2 * count + half :]

    feature = lax.broadcasted_iota(jnp.int32, (BLOCK, BLOCK), 0) - WIDTH
    which = lax.broadcasted_iota(jnp.int32, (BLOCK, BLOCK), 1) // LANES
    for unit in range(2):
        axis = which + 2 * unit
        pick = (feature == 5 + axis) | (feature == 16 + axis) | (feature == 25 + axis)
        pltpu.matmul_push_rhs((pick & (axis < 3)).astype(F32).astype(BF16), 0, unit)
    pltpu.matmul_acc_lhs(radius_acc[0], left_m[0:PIECE, :], load_staged_rhs=0)
    pltpu.matmul_acc_lhs(coupling_acc[0], left_m[0:PIECE, :], load_staged_rhs=0)
    pltpu.matmul_pop(radius_acc[0])
    pltpu.matmul_pop(coupling_acc[0])

    def spread_prep(i, _):
        for p in range(count):
            left = left_m[pl.ds(pl.multiple_of(i * CHUNK + p * PIECE, PIECE), PIECE), :]
            pltpu.matmul_acc_lhs(radius_acc[p], left)
            pltpu.matmul_acc_lhs(coupling_acc[p], left)
        for p in range(count):
            at = pl.ds(pl.multiple_of(i * CHUNK + p * PIECE, PIECE), PIECE)
            spread[at, 0 : 2 * LANES] = pltpu.matmul_pop(radius_acc[p])
            spread[at, 2 * LANES :] = pltpu.matmul_pop(coupling_acc[p])[:, 0:LANES]
            tgt_sum[at, :] = jnp.zeros((PIECE, 3 * LANES), F32)
        return 0

    lax.fori_loop(0, chunks, spread_prep, 0)

    zeros = jnp.zeros((WIDTH, BLOCK), BF16)

    def source_prep(b, _):
        for h in range(halves):
            pack = packs[b, :, h * BLOCK : (h + 1) * BLOCK]
            block = b * halves + h
            density = pack[0:WIDTH]
            pos = pack[WIDTH : WIDTH + 3]
            nrm = pack[WIDTH + 3 : WIDTH + 6]
            scaled = density * (pack[WIDTH + 6 : WIDTH + 7] * INV_FOUR_PI)
            high = scaled.astype(BF16)
            low = (scaled - high.astype(F32)).astype(BF16)
            radius, normal = source_features(pos, nrm)
            for q, quarters in enumerate((
                (high, zeros, high, low),
                (zeros, radius.astype(BF16), zeros, zeros),
                (zeros, normal.astype(BF16), zeros, zeros),
            )):
                for r, quarter in enumerate(quarters):
                    right_m[block, q, r * WIDTH : (r + 1) * WIDTH, :] = quarter
            src_rows[block] = pack[WIDTH : WIDTH + 8]
            src_sum[block] = jnp.zeros(src_sum.shape[1:], F32)
            stacked = jnp.concatenate([density, rows([nrm], WIDTH)], axis=0)
            src_table[pl.ds(pl.multiple_of(block * BLOCK, BLOCK), BLOCK), :] = jnp.transpose(stacked)
        return 0

    lax.fori_loop(0, parts, source_prep, 0)

    steps = blocks * chunks

    def where(k):
        k = jnp.minimum(k, steps - 1)
        return k // chunks, lax.rem(k, chunks)

    def enter(e, k):
        b, i = where(k)

        def left(p):
            return left_m[pl.ds(pl.multiple_of(i * CHUNK + p * PIECE, PIECE), PIECE), :]

        if e == 0:
            pltpu.matmul_push_rhs(right_m[b, 1], 0, 0)
            pltpu.matmul_push_rhs(right_m[b, 0], 0, 1)
        if e == count:
            pltpu.matmul_push_rhs(right_m[b, 2], 1, 0)
            pltpu.matmul_push_rhs(right_m[b, 2], 1, 1)
        if e < count:
            load = 0 if e == 0 else None
            pltpu.matmul_acc_lhs(radius_acc[e], left(e), load_staged_rhs=load)
            pltpu.matmul_acc_lhs(coupling_acc[e], left(e), load_staged_rhs=load)
        else:
            load = 1 if e == count else None
            pltpu.matmul_acc_lhs(first_acc[e - count], left(e - count), load_staged_rhs=load)
            pltpu.matmul_acc_lhs(second_acc[e - count], left(e - half), load_staged_rhs=load)

    def leave(e, buf):
        if e < count:
            at = slice(e * PIECE, (e + 1) * PIECE)
            buf[at, BLOCK : 2 * BLOCK] = pltpu.matmul_pop(radius_acc[e])
            buf[at, 0:BLOCK] = pltpu.matmul_pop(coupling_acc[e])
        else:
            for p, acc in ((e - count, first_acc[e - count]), (e - half, second_acc[e - count])):
                buf[p * PIECE : (p + 1) * PIECE, 2 * BLOCK : 3 * BLOCK] = pltpu.matmul_pop(acc)

    events = count + half
    per_step = pairs // steps

    def pick_pair(p):
        t = near_tgt[p] - first_target
        product[pl.ds(p, 1), :] = held[pl.ds(t, 1), :] * src_table[pl.ds(near_src[p], 1), :]

    def sums(k, buf, after):
        b, i = where(k)
        base = i * CHUNK
        src = src_rows[b]
        wide = BLOCK // LANES
        lane = [slice(j * LANES, (j + 1) * LANES) for j in range(wide)]
        row = [[jnp.broadcast_to(src[q : q + 1, lane[j]], (8, LANES)) for q in range(6)] for j in range(wide)]
        groups = CHUNK // 8
        acc = None
        for r in range(groups):
            for e in range(events):
                if e * groups // events == r:
                    leave(e, after)
                    enter(e, k + 2)
            for u in range(per_step):
                if u * groups // per_step == r:
                    pick_pair(k * per_step + u)
            if r % GROUP == 0:
                acc = [[None] * 3 for _ in range(wide)]
            at = pl.ds(pl.multiple_of(base + 8 * r, 8), 8)
            here = [spread[at, c * LANES : (c + 1) * LANES] for c in range(3)]
            total_t = [None] * 3
            for j in range(wide):
                cols = slice(8 * r, 8 * r + 8)
                coupling = buf[cols, j * LANES : (j + 1) * LANES]
                radius = buf[cols, BLOCK + j * LANES : BLOCK + (j + 1) * LANES]
                normal = buf[cols, 2 * BLOCK + j * LANES : 2 * BLOCK + (j + 1) * LANES]
                inv = lax.rsqrt(radius)
                inv2 = inv * inv
                scale = (coupling * inv) * inv2
                along = normal * inv2
                for c in range(3):
                    g = scale * (row[j][3 + c] - along * (here[c] - row[j][c]))
                    acc[j][c] = g if acc[j][c] is None else acc[j][c] + g
                    total_t[c] = g if total_t[c] is None else total_t[c] + g
            for c in range(3):
                tgt_sum[at, c * LANES : (c + 1) * LANES] += total_t[c]
            if r % GROUP == GROUP - 1:
                for j in range(wide):
                    for c in range(3):
                        src_sum[b, r // GROUP, 8 * c : 8 * c + 8, lane[j]] += acc[j][c]

    for e in range(events):
        enter(e, 0)
    for e in range(events):
        leave(e, buf0)
        enter(e, 1)

    once = jnp.where(near_src[0] >= 0, 1, 0)

    def far(h, _):
        lax.fori_loop(0, once, lambda z, c: (sums(2 * h, buf0, buf1), c)[1], 0)
        lax.fori_loop(0, once, lambda z, c: (sums(2 * h + 1, buf1, buf0), c)[1], 0)
        return 0

    lax.fori_loop(0, steps // 2, far, 0)
    for e in range(events):
        leave(e, buf0)

    flat = jnp.transpose(product[...])
    coupled = jnp.sum(flat[0:WIDTH], axis=0, keepdims=True) * near_coef[...]
    value = coupled * flat[WIDTH : WIDTH + 3]
    high = part(value)
    both = rows([high, part(value - high)], 8)

    def scatter(index, unit, acc):
        row_at, lane_at = index // BLOCK, lax.rem(index, BLOCK)
        picked = [jnp.where(row_at == g, both, 0.0) for g in range(4 * len(acc))]
        picked = jnp.concatenate(picked, axis=0).astype(BF16)
        lanes = (lax.broadcasted_iota(jnp.int32, (BLOCK, pairs), 0) == lane_at).astype(F32).astype(BF16)
        for q in range(pairs // BLOCK):
            at = slice(q * BLOCK, (q + 1) * BLOCK)
            pltpu.matmul_push_rhs(lanes[:, at], q % 2, unit, transpose=True)
            for p in range(len(acc)):
                load = q % 2 if p == 0 else None
                pltpu.matmul_acc_lhs(acc[p], picked[p * PIECE : (p + 1) * PIECE, at], load_staged_rhs=load)
        return jnp.concatenate([pltpu.matmul_pop(one) for one in acc], axis=0)

    local = near_tgt_row[...] - first_target
    to_tgt = scatter(local, 0, radius_acc[0 : tgt_count // BLOCK // 4])
    to_src = scatter(near_src_row[...], 1, coupling_acc[0 : total // BLOCK // 4])
    wide = BLOCK // LANES

    def near_of(sums_by_row, g):
        near = sums_by_row[8 * (g // wide) : 8 * (g // wide) + 8, g % wide * LANES : (g % wide + 1) * LANES]
        return near[0:3] + near[3:6]

    lane = lax.broadcasted_iota(jnp.int32, (LANES, LANES), 1)
    for g in range(tgt_count // LANES):
        at = slice(g * LANES, (g + 1) * LANES)
        merged = jnp.zeros((LANES, LANES), F32)
        for c in range(3):
            one = jnp.sum(tgt_sum[at, c * LANES : (c + 1) * LANES], axis=1, keepdims=True)
            merged = jnp.where(lane == c, one, merged)
        tgt_out[:, at] = jnp.transpose(merged)[0:3] + near_of(to_tgt, g)
    quarters = per // LANES
    for b in range(parts):
        src_out[b, 3 * quarters :, :] = jnp.zeros((src_out.shape[1] - 3 * quarters, LANES), F32)
        for q in range(quarters):
            g = b * quarters + q
            block, j = divmod(g, BLOCK // LANES)
            near = near_of(to_src, g)
            at = slice(j * LANES, (j + 1) * LANES)
            together = sum(src_sum[block, s, :, at] for s in range(src_sum.shape[1]))
            for c in range(3):
                far_sum = jnp.sum(together[8 * c : 8 * c + 8], axis=0, keepdims=True)
                row = c * quarters + q
                src_out[b, row : row + 1, :] = -far_sum - near[c : c + 1]


def pair_sums(tgt_pos, tgt_area, tgt_cond, adjoint, cond_scale, near_tgt, near_src, near_coef, packs):
    tgt_count = tgt_pos.shape[1]
    pairs = near_coef.shape[0]
    parts, _, per = packs.shape
    total = parts * per
    blocks = total // BLOCK
    vmem = pl.BlockSpec(memory_space=pltpu.VMEM)
    smem = pl.BlockSpec(memory_space=pltpu.SMEM)
    return pl.pallas_call(
        pair_kernel,
        out_shape=[
            jax.ShapeDtypeStruct((3, tgt_count), F32),
            jax.ShapeDtypeStruct((parts, SUM_ROWS, LANES), F32),
        ],
        in_specs=[smem, smem] + [vmem] * 9,
        out_specs=[vmem, vmem],
        scratch_shapes=[
            pltpu.VMEM((tgt_count, LANES), F32),
            pltpu.VMEM((tgt_count, 2 * LANES), BF16),
            pltpu.VMEM((blocks, 3, BLOCK, BLOCK), BF16),
            pltpu.VMEM((blocks, 8, BLOCK), F32),
            pltpu.VMEM((total, LANES), F32),
            pltpu.VMEM((tgt_count, 3 * LANES), F32),
            pltpu.VMEM((tgt_count, 3 * LANES), F32),
            pltpu.VMEM((blocks, CHUNK // 8 // GROUP, 24, BLOCK), F32),
            pltpu.VMEM((pairs, LANES), F32),
            pltpu.VMEM((CHUNK, 3 * BLOCK), F32),
            pltpu.VMEM((CHUNK, 3 * BLOCK), F32),
        ],
        compiler_params=pltpu.CompilerParams(vmem_limit_bytes=60 * 2**20),
    )(
        near_tgt, near_src, tgt_pos, tgt_area[None, :], tgt_cond[None, :], adjoint, jnp.pad(cond_scale, (0, LANES - WIDTH))[None, :],
        near_tgt[None, :], near_src[None, :], near_coef[None, :], packs,
    )


def greet(peers):
    barrier = pltpu.get_barrier_semaphore()
    for peer in peers:
        pl.semaphore_signal(barrier, inc=1, device_id=peer, device_id_type=MESH)
    pl.semaphore_wait(barrier, len(peers))


def gather_kernel(density, pos, nrm, area, out, pack, send_sem, recv_sem, local_sem):
    me, grp = lax.axis_index("blk"), lax.axis_index("grp")
    z, y_lo, core = me // 4, lax.rem(me // 2, 2), lax.rem(me, 2)

    def block(z_at, y_at, core_at):
        return (lax.rem(z_at, 4) * 2 + y_at) * 2 + core_at

    up, down = block(z + 1, y_lo, core), block(z + 3, y_lo, core)
    beside, mate = block(z, 1 - y_lo, core), block(z, y_lo, 1 - core)
    other = grp + 1 - 2 * lax.rem(grp, 2)
    to_up, to_down, to_mate = {"blk": up}, {"blk": down}, {"blk": mate}
    to_beside, to_around = {"blk": beside}, {"blk": beside, "grp": other}

    width = density.shape[0]
    pack[0:width, :] = density[...]
    pack[width:, :] = jnp.concatenate(
        [pos[...], nrm[...], area[...], jnp.zeros((PACK - width - 7, pos.shape[1]), F32)], axis=0
    )
    greet([to_up, to_down, to_mate, to_beside, to_around])

    whole, first, second = pl.ds(0, PACK), pl.ds(0, 40), pl.ds(40, PACK - 40)
    copies = {}

    def send(name, source, piece, device):
        k = len(copies)
        held = pack if source is me else out.at[source]
        copy = pltpu.make_async_remote_copy(
            src_ref=held.at[piece], dst_ref=out.at[source, piece], send_sem=send_sem.at[k], recv_sem=recv_sem.at[k],
            device_id=device, device_id_type=MESH,
        )
        copy.start()
        copies[name] = copy

    def spread_y(name, source):
        send(name + "first", source, first, to_beside)
        send(name + "second", source, second, to_around)

    def arrived(*names):
        for name in names:
            copies[name].wait_recv()

    send("up", me, whole, to_up)
    send("down", me, whole, to_down)
    spread_y("y0", me)
    send("c0", me, whole, to_mate)
    mine = pltpu.make_async_copy(pack, out.at[me], local_sem)
    mine.start()
    arrived("up")
    send("up2", down, first, to_up)
    spread_y("y3", down)
    send("c3", down, whole, to_mate)
    arrived("down")
    send("down2", up, second, to_down)
    spread_y("y1", up)
    send("c1", up, whole, to_mate)
    across = block(z + 2, y_lo, core)
    arrived("up2", "down2")
    spread_y("y2", across)
    send("c2", across, whole, to_mate)
    for step in (0, 3, 1, 2):
        arrived("y%dfirst" % step, "y%dsecond" % step)
        send("cy%d" % step, block(z + step, 1 - y_lo, core), whole, to_mate)
    for step in (0, 3, 1, 2):
        arrived("c%d" % step)
    for step in (0, 3, 1, 2):
        arrived("cy%d" % step)
    mine.wait()
    for copy in copies.values():
        copy.wait_send()


def gather_sources(density, pos, nrm, area, n):
    vmem, hbm = pl.BlockSpec(memory_space=pltpu.VMEM), pl.BlockSpec(memory_space=pl.ANY)
    shape = (PACK, pos.shape[1])
    return pl.pallas_call(
        gather_kernel,
        out_shape=jax.ShapeDtypeStruct((n,) + shape, F32),
        in_specs=[vmem] * 4,
        out_specs=hbm,
        scratch_shapes=[
            pltpu.VMEM(shape, F32),
            pltpu.SemaphoreType.DMA((20,)),
            pltpu.SemaphoreType.DMA((20,)),
            pltpu.SemaphoreType.DMA,
        ],
        compiler_params=pltpu.CompilerParams(collective_id=0, has_side_effects=True),
    )(density, pos, nrm, area[None, :])


def reduce_kernel(n, groups, sums, out, first, second, mine, send1, recv1, send2, recv2):
    me, grp = lax.axis_index("blk"), lax.axis_index("grp")
    blk_others = [lax.rem(me + k, n) for k in range(1, n)]
    grp_others = [lax.rem(grp + k, groups) for k in range(1, groups)]
    greet([{"blk": other} for other in blk_others] + [{"grp": other} for other in grp_others])
    copies = []
    for k, other in enumerate(blk_others):
        copy = pltpu.make_async_remote_copy(
            src_ref=sums.at[other], dst_ref=first.at[k], send_sem=send1.at[k], recv_sem=recv1.at[k],
            device_id={"blk": other}, device_id_type=MESH,
        )
        copy.start()
        copies.append(copy)
    total = sums[me]
    for k, copy in enumerate(copies):
        copy.wait_recv()
        total = total + first[k]
    quarters = groups // 2
    for q in range(quarters):
        mine[q] = jnp.concatenate(
            [total[c * quarters + q : c * quarters + q + 1] for c in range(3)] + [jnp.zeros((5, LANES), F32)], axis=0
        )
    more = []
    for k, other in enumerate(grp_others):
        copy = pltpu.make_async_remote_copy(
            src_ref=mine.at[other // 2], dst_ref=second.at[k], send_sem=send2.at[k], recv_sem=recv2.at[k],
            device_id={"grp": other}, device_id_type=MESH,
        )
        copy.start()
        more.append(copy)
    result = mine[grp // 2]
    for k, copy in enumerate(more):
        copy.wait_recv()
        result = result + second[k]
    half = LANES // 2
    out[...] = jnp.where(lax.rem(grp, 2) == 1, result[0:3, half:], result[0:3, 0:half])
    for copy in copies + more:
        copy.wait_send()


def reduce_sources(sums, n, groups):
    vmem = pl.BlockSpec(memory_space=pltpu.VMEM)
    return pl.pallas_call(
        functools.partial(reduce_kernel, n, groups),
        out_shape=jax.ShapeDtypeStruct((3, LANES // 2), F32),
        in_specs=[vmem],
        out_specs=vmem,
        scratch_shapes=[
            pltpu.VMEM((n - 1, SUM_ROWS, LANES), F32),
            pltpu.VMEM((groups - 1, 8, LANES), F32),
            pltpu.VMEM((groups // 2, 8, LANES), F32),
            pltpu.SemaphoreType.DMA((n - 1,)),
            pltpu.SemaphoreType.DMA((n - 1,)),
            pltpu.SemaphoreType.DMA((groups - 1,)),
            pltpu.SemaphoreType.DMA((groups - 1,)),
        ],
        compiler_params=pltpu.CompilerParams(collective_id=1, has_side_effects=True),
    )(sums)


def per_device(
    tgt_pos, tgt_area, tgt_cond, adjoint, src_pos, src_nrm, src_area, density, cond_scale, near_tgt, near_src, near_coef
):
    n, groups = lax.axis_size("blk"), lax.axis_size("grp")
    packs = gather_sources(density, src_pos, src_nrm, src_area, n)
    tgt_grad, sums = pair_sums(
        tgt_pos, tgt_area, tgt_cond, adjoint, cond_scale, near_tgt, near_src, near_coef, packs
    )
    return tgt_grad, reduce_sources(sums, n, groups)


def solution(mesh):
    placed = (
        P(None, ("blk", "grp")),
        P(("blk", "grp")),
        P(("blk", "grp")),
        P(None, ("blk", "grp")),
        P(None, "blk"),
        P(None, "blk"),
        P("blk"),
        P(None, "blk"),
        P(),
        P(("blk", "grp")),
        P(("blk", "grp")),
        P(("blk", "grp")),
    )
    return jax.shard_map(
        per_device,
        mesh=mesh,
        in_specs=placed,
        out_specs=(P(None, ("blk", "grp")), P(None, ("blk", "grp"))),
        check_vma=False,
    )
```

```python
import functools
import math

import jax
import jax.numpy as jnp
from jax import lax
from jax.experimental import pallas as pl
from jax.experimental.pallas import tpu as pltpu
from jax.sharding import PartitionSpec as P

SOFTEN = 0.05
INV_FOUR_PI = 1.0 / (4.0 * math.pi)
MESH = pl.DeviceIdType.MESH
F32 = jnp.float32
BF16 = jnp.bfloat16
LANES = 128
WIDTH = 64
PACK = 72
BLOCK = 256
CHUNK = 512
PIECE = 32
GROUP = 32
SUM_ROWS = 16


def part(x):
    return x.astype(BF16).astype(F32)


def three_parts(x):
    first = part(x)
    second = part(x - first)
    return first, second, part(x - first - second)


def grid_parts(x):
    first = jnp.floor(x * 16.0 + 0.5) * 0.0625
    rest = x - first
    second = part(rest)
    return first, second, part(rest - second), rest


def square_parts(first, rest):
    square = jnp.sum(first * first, axis=0, keepdims=True)
    whole = jnp.floor(square)
    left = jnp.sum((2.0 * first + rest) * rest, axis=0, keepdims=True)
    return whole, square - whole, left


def rows(pieces, total):
    count = sum(p.shape[0] for p in pieces)
    width = pieces[0].shape[1]
    if count < total:
        pieces = list(pieces) + [jnp.zeros((total - count, width), F32)]
    return jnp.concatenate(pieces, axis=0)


def target_features(pos):
    t1, t2, t3, rest = grid_parts(pos)
    whole, fraction, left = square_parts(t1, rest)
    ones = jnp.ones((5, pos.shape[1]), F32)
    return rows([ones, t1, whole, fraction, t1, t1, t2, t2, t2, t3, t3, *three_parts(left)], WIDTH)


def source_features(pos, nrm):
    s1, s2, s3, rest = grid_parts(pos)
    whole, fraction, left = square_parts(s1, rest)
    zero = jnp.zeros((1, pos.shape[1]), F32)
    one = jnp.ones((1, pos.shape[1]), F32)
    radius = rows(
        [whole, fraction, *three_parts(left + SOFTEN)]
        + [-2.0 * s1, one, one, -2.0 * s2, -2.0 * s3, -2.0 * s1, -2.0 * s2, -2.0 * s3, -2.0 * s1, -2.0 * s2]
        + [one, one, one],
        WIDTH,
    )
    triple = 3.0 * nrm
    n1, n2, n3 = three_parts(triple)
    offset = -jnp.sum(triple * pos, axis=0, keepdims=True)
    normal = rows(
        [*three_parts(offset), zero, zero]
        + [n1, zero, zero, n2, n3, n1, n2, n3, n1, n2]
        + [zero, zero, zero],
        WIDTH,
    )
    return radius, normal


def pair_kernel(*refs):
    pieces = CHUNK // PIECE
    units = [pltpu.ACC(unit)((PIECE, BLOCK), F32) for unit in range(2) for _ in range(pieces + pieces // 2)]
    pl.run_scoped(lambda *accs: pair_body(accs, *refs), *units)


def pair_body(
    accs,
    near_tgt, near_src, tgt_pos, tgt_area, tgt_cond, adjoint, cond_scale, near_tgt_row, near_src_row, near_coef, packs_in,
    tgt_out, src_out,
    packs, packs_sem, held, left_m, right_m, src_rows, src_table, spread, tgt_sum, src_sum, product, buf0, buf1,
):
    fetch = pltpu.make_async_copy(packs_in, packs, packs_sem)
    fetch.start()
    tgt_count = tgt_pos.shape[1]
    parts, _, per = packs.shape
    total = parts * per
    halves = per // BLOCK
    blocks = total // BLOCK
    chunks = tgt_count // CHUNK
    pairs = near_coef.shape[1]
    first_target = (near_tgt[0] // tgt_count) * tgt_count

    scales = jnp.concatenate([cond_scale[...], jnp.zeros((1, LANES - WIDTH), F32)], axis=1)
    scales = jnp.transpose(jnp.broadcast_to(scales, (LANES, LANES)))[0:WIDTH]
    scales = jnp.concatenate([scales] * (CHUNK // LANES), axis=1)

    def target_prep(i, _):
        cols = pl.ds(pl.multiple_of(i * CHUNK, CHUNK), CHUNK)
        hit = lax.broadcasted_iota(jnp.int32, (WIDTH, CHUNK), 0) == tgt_cond[:, cols]
        weight = tgt_area[:, cols] * jnp.sum(jnp.where(hit, scales, 0.0), axis=0, keepdims=True)
        stacked = jnp.concatenate([adjoint[:, cols] * weight, target_features(tgt_pos[:, cols])], axis=0)
        flat = jnp.transpose(stacked)
        held[cols, :] = flat
        high = part(flat)
        low = flat - high
        lane = lax.broadcasted_iota(jnp.int32, (CHUNK, LANES), 1)
        second = jnp.where(lane >= WIDTH, pltpu.roll(high, WIDTH, 1), low)
        left_m[cols, 0:LANES] = high.astype(BF16)
        left_m[cols, LANES : 2 * LANES] = second.astype(BF16)
        return 0

    lax.fori_loop(0, chunks, target_prep, 0)

    count = CHUNK // PIECE
    half = count // 2
    radius_acc, first_acc = accs[0:count], accs[count : count + half]
    coupling_acc, second_acc = accs[count + half : 2 * count + half], accs[2 * count + half :]

    feature = lax.broadcasted_iota(jnp.int32, (BLOCK, BLOCK), 0) - WIDTH
    which = lax.broadcasted_iota(jnp.int32, (BLOCK, BLOCK), 1) // LANES
    for unit in range(2):
        axis = which + 2 * unit
        pick = (feature == 5 + axis) | (feature == 16 + axis) | (feature == 25 + axis)
        pltpu.matmul_push_rhs((pick & (axis < 3)).astype(F32).astype(BF16), 0, unit)
    pltpu.matmul_acc_lhs(radius_acc[0], left_m[0:PIECE, :], load_staged_rhs=0)
    pltpu.matmul_acc_lhs(coupling_acc[0], left_m[0:PIECE, :], load_staged_rhs=0)
    pltpu.matmul_pop(radius_acc[0])
    pltpu.matmul_pop(coupling_acc[0])

    def spread_prep(i, _):
        for p in range(count):
            left = left_m[pl.ds(pl.multiple_of(i * CHUNK + p * PIECE, PIECE), PIECE), :]
            pltpu.matmul_acc_lhs(radius_acc[p], left)
            pltpu.matmul_acc_lhs(coupling_acc[p], left)
        for p in range(count):
            at = pl.ds(pl.multiple_of(i * CHUNK + p * PIECE, PIECE), PIECE)
            spread[at, 0 : 2 * LANES] = pltpu.matmul_pop(radius_acc[p])
            spread[at, 2 * LANES :] = pltpu.matmul_pop(coupling_acc[p])[:, 0:LANES]
            tgt_sum[at, :] = jnp.zeros((PIECE, 3 * LANES), F32)
        return 0

    lax.fori_loop(0, chunks, spread_prep, 0)

    zeros = jnp.zeros((WIDTH, BLOCK), BF16)

    def source_prep(b, _):
        for h in range(halves):
            pack = packs[b, :, h * BLOCK : (h + 1) * BLOCK]
            block = b * halves + h
            density = pack[0:WIDTH]
            pos = pack[WIDTH : WIDTH + 3]
            nrm = pack[WIDTH + 3 : WIDTH + 6]
            scaled = density * (pack[WIDTH + 6 : WIDTH + 7] * INV_FOUR_PI)
            high = scaled.astype(BF16)
            low = (scaled - high.astype(F32)).astype(BF16)
            radius, normal = source_features(pos, nrm)
            for q, quarters in enumerate((
                (high, zeros, high, low),
                (zeros, radius.astype(BF16), zeros, zeros),
                (zeros, normal.astype(BF16), zeros, zeros),
            )):
                for r, quarter in enumerate(quarters):
                    right_m[block, q, r * WIDTH : (r + 1) * WIDTH, :] = quarter
            src_rows[block] = pack[WIDTH : WIDTH + 8]
            src_sum[block] = jnp.zeros(src_sum.shape[1:], F32)
            stacked = jnp.concatenate([density, rows([nrm], WIDTH)], axis=0)
            src_table[pl.ds(pl.multiple_of(block * BLOCK, BLOCK), BLOCK), :] = jnp.transpose(stacked)
        return 0

    fetch.wait()
    lax.fori_loop(0, parts, source_prep, 0)

    steps = blocks * chunks

    def where(k):
        k = jnp.minimum(k, steps - 1)
        return k // chunks, lax.rem(k, chunks)

    def turn(e, unit, odd):
        if unit == 0:
            whole = [(1, p, radius_acc[p]) for p in range(count)]
            part_of = [(2, p, first_acc[p]) for p in range(half)]
        else:
            whole = [(0, p, coupling_acc[p]) for p in range(count)]
            part_of = [(2, p + half, second_acc[p]) for p in range(half)]
        order = whole + part_of if unit == odd else part_of + whole
        change = len(whole) if unit == odd else len(part_of)
        return order[e] + (e == change or (e == 0 and odd == 0),)

    def enter(e, k, unit, odd):
        b, i = where(k)
        matrix, p, acc, first = turn(e, unit, odd)
        staged = 1 if matrix == 2 else 0
        if first:
            pltpu.matmul_push_rhs(right_m[b, matrix], staged, unit)
        left = left_m[pl.ds(pl.multiple_of(i * CHUNK + p * PIECE, PIECE), PIECE), :]
        pltpu.matmul_acc_lhs(acc, left, load_staged_rhs=staged if first else None)

    def leave(e, buf, unit, odd):
        matrix, p, acc, _ = turn(e, unit, odd)
        buf[p * PIECE : (p + 1) * PIECE, matrix * BLOCK : (matrix + 1) * BLOCK] = pltpu.matmul_pop(acc)

    events = count + half
    per_step = pairs // steps

    def pick_pair(p):
        t = near_tgt[p] - first_target
        product[pl.ds(p, 1), :] = held[pl.ds(t, 1), :] * src_table[pl.ds(near_src[p], 1), :]

    def sums(k, buf, after, odd):
        b, i = where(k)
        base = i * CHUNK
        src = src_rows[b]
        wide = BLOCK // LANES
        lane = [slice(j * LANES, (j + 1) * LANES) for j in range(wide)]
        row = [[jnp.broadcast_to(src[q : q + 1, lane[j]], (8, LANES)) for q in range(6)] for j in range(wide)]
        groups = CHUNK // 8
        acc = None
        for r in range(groups):
            for unit in range(2):
                for e in range(events):
                    if (2 * e + unit) * groups // (2 * events) == r:
                        leave(e, after, unit, odd)
                        enter(e, k + 2, unit, odd)
            for u in range(per_step):
                if u * groups // per_step == r:
                    pick_pair(k * per_step + u)
            if r % GROUP == 0:
                acc = [[None] * 3 for _ in range(wide)]
            at = pl.ds(pl.multiple_of(base + 8 * r, 8), 8)
            here = [spread[at, c * LANES : (c + 1) * LANES] for c in range(3)]
            total_t = [None] * 3
            for j in range(wide):
                cols = slice(8 * r, 8 * r + 8)
                coupling = buf[cols, j * LANES : (j + 1) * LANES]
                radius = buf[cols, BLOCK + j * LANES : BLOCK + (j + 1) * LANES]
                normal = buf[cols, 2 * BLOCK + j * LANES : 2 * BLOCK + (j + 1) * LANES]
                inv = lax.rsqrt(radius)
                inv2 = inv * inv
                scale = (coupling * inv) * inv2
                along = normal * inv2
                for c in range(3):
                    g = scale * (row[j][3 + c] - along * (here[c] - row[j][c]))
                    acc[j][c] = g if acc[j][c] is None else acc[j][c] + g
                    total_t[c] = g if total_t[c] is None else total_t[c] + g
            for c in range(3):
                tgt_sum[at, c * LANES : (c + 1) * LANES] += total_t[c]
            if r % GROUP == GROUP - 1:
                for j in range(wide):
                    for c in range(3):
                        src_sum[b, r // GROUP, 8 * c : 8 * c + 8, lane[j]] += acc[j][c]

    for unit in range(2):
        for e in range(events):
            enter(e, 0, unit, 0)
    for unit in range(2):
        for e in range(events):
            leave(e, buf0, unit, 1)
            enter(e, 1, unit, 1)

    once = jnp.where(near_src[0] >= 0, 1, 0)

    def far(h, _):
        lax.fori_loop(0, once, lambda z, c: (sums(2 * h, buf0, buf1, 0), c)[1], 0)
        lax.fori_loop(0, once, lambda z, c: (sums(2 * h + 1, buf1, buf0, 1), c)[1], 0)
        return 0

    lax.fori_loop(0, steps // 2, far, 0)
    for unit in range(2):
        for e in range(events):
            leave(e, buf0, unit, 0)

    flat = jnp.transpose(product[...])
    coupled = jnp.sum(flat[0:WIDTH], axis=0, keepdims=True) * near_coef[...]
    value = coupled * flat[WIDTH : WIDTH + 3]
    high = part(value)
    both = rows([high, part(value - high)], 8)

    def scatter(index, unit, acc):
        row_at, lane_at = index // BLOCK, lax.rem(index, BLOCK)
        picked = [jnp.where(row_at == g, both, 0.0) for g in range(4 * len(acc))]
        picked = jnp.concatenate(picked, axis=0).astype(BF16)
        lanes = (lax.broadcasted_iota(jnp.int32, (BLOCK, pairs), 0) == lane_at).astype(F32).astype(BF16)
        for q in range(pairs // BLOCK):
            at = slice(q * BLOCK, (q + 1) * BLOCK)
            pltpu.matmul_push_rhs(lanes[:, at], q % 2, unit, transpose=True)
            for p in range(len(acc)):
                load = q % 2 if p == 0 else None
                pltpu.matmul_acc_lhs(acc[p], picked[p * PIECE : (p + 1) * PIECE, at], load_staged_rhs=load)
        return jnp.concatenate([pltpu.matmul_pop(one) for one in acc], axis=0)

    local = near_tgt_row[...] - first_target
    to_tgt = scatter(local, 0, radius_acc[0 : tgt_count // BLOCK // 4])
    to_src = scatter(near_src_row[...], 1, coupling_acc[0 : total // BLOCK // 4])
    wide = BLOCK // LANES

    def near_of(sums_by_row, g):
        near = sums_by_row[8 * (g // wide) : 8 * (g // wide) + 8, g % wide * LANES : (g % wide + 1) * LANES]
        return near[0:3] + near[3:6]

    lane = lax.broadcasted_iota(jnp.int32, (LANES, LANES), 1)
    for g in range(tgt_count // LANES):
        at = slice(g * LANES, (g + 1) * LANES)
        merged = jnp.zeros((LANES, LANES), F32)
        for c in range(3):
            one = jnp.sum(tgt_sum[at, c * LANES : (c + 1) * LANES], axis=1, keepdims=True)
            merged = jnp.where(lane == c, one, merged)
        tgt_out[:, at] = jnp.transpose(merged)[0:3] + near_of(to_tgt, g)
    quarters = per // LANES
    for b in range(parts):
        src_out[b, 3 * quarters :, :] = jnp.zeros((src_out.shape[1] - 3 * quarters, LANES), F32)
        for q in range(quarters):
            g = b * quarters + q
            block, j = divmod(g, BLOCK // LANES)
            near = near_of(to_src, g)
            at = slice(j * LANES, (j + 1) * LANES)
            together = sum(src_sum[block, s, :, at] for s in range(src_sum.shape[1]))
            for c in range(3):
                far_sum = jnp.sum(together[8 * c : 8 * c + 8], axis=0, keepdims=True)
                row = c * quarters + q
                src_out[b, row : row + 1, :] = -far_sum - near[c : c + 1]


def pair_sums(tgt_pos, tgt_area, tgt_cond, adjoint, cond_scale, near_tgt, near_src, near_coef, packs):
    tgt_count = tgt_pos.shape[1]
    pairs = near_coef.shape[0]
    parts, _, per = packs.shape
    total = parts * per
    blocks = total // BLOCK
    vmem = pl.BlockSpec(memory_space=pltpu.VMEM)
    smem = pl.BlockSpec(memory_space=pltpu.SMEM)
    return pl.pallas_call(
        pair_kernel,
        out_shape=[
            jax.ShapeDtypeStruct((3, tgt_count), F32),
            jax.ShapeDtypeStruct((parts, SUM_ROWS, LANES), F32),
        ],
        in_specs=[smem, smem] + [vmem] * 8 + [pl.BlockSpec(memory_space=pl.ANY)],
        out_specs=[vmem, vmem],
        scratch_shapes=[
            pltpu.VMEM(packs.shape, F32),
            pltpu.SemaphoreType.DMA,
            pltpu.VMEM((tgt_count, LANES), F32),
            pltpu.VMEM((tgt_count, 2 * LANES), BF16),
            pltpu.VMEM((blocks, 3, BLOCK, BLOCK), BF16),
            pltpu.VMEM((blocks, 8, BLOCK), F32),
            pltpu.VMEM((total, LANES), F32),
            pltpu.VMEM((tgt_count, 3 * LANES), F32),
            pltpu.VMEM((tgt_count, 3 * LANES), F32),
            pltpu.VMEM((blocks, CHUNK // 8 // GROUP, 24, BLOCK), F32),
            pltpu.VMEM((pairs, LANES), F32),
            pltpu.VMEM((CHUNK, 3 * BLOCK), F32),
            pltpu.VMEM((CHUNK, 3 * BLOCK), F32),
        ],
        compiler_params=pltpu.CompilerParams(vmem_limit_bytes=60 * 2**20),
    )(
        near_tgt, near_src, tgt_pos, tgt_area[None, :], tgt_cond[None, :], adjoint, cond_scale[None, :],
        near_tgt[None, :], near_src[None, :], near_coef[None, :], packs,
    )


def greet(peers):
    barrier = pltpu.get_barrier_semaphore()
    for peer in peers:
        pl.semaphore_signal(barrier, inc=1, device_id=peer, device_id_type=MESH)
    pl.semaphore_wait(barrier, len(peers))


def gather_kernel(density, pos, nrm, area, out, pack, send_sem, recv_sem, local_sem):
    me, grp = lax.axis_index("blk"), lax.axis_index("grp")
    z, y_lo, core = me // 4, lax.rem(me // 2, 2), lax.rem(me, 2)

    def block(z_at, y_at, core_at):
        return (lax.rem(z_at, 4) * 2 + y_at) * 2 + core_at

    up, down = block(z + 1, y_lo, core), block(z + 3, y_lo, core)
    beside, mate = block(z, 1 - y_lo, core), block(z, y_lo, 1 - core)
    other = grp + 1 - 2 * lax.rem(grp, 2)
    to_up, to_down, to_mate = {"blk": up}, {"blk": down}, {"blk": mate}
    to_beside, to_around = {"blk": beside}, {"blk": beside, "grp": other}

    width = density.shape[0]
    pack[0:width, :] = density[...]
    pack[width:, :] = jnp.concatenate(
        [pos[...], nrm[...], area[...], jnp.zeros((PACK - width - 7, pos.shape[1]), F32)], axis=0
    )
    greet([to_up, to_down, to_mate, to_beside, to_around])

    whole, first, second = pl.ds(0, PACK), pl.ds(0, 40), pl.ds(40, PACK - 40)
    copies = {}

    def send(name, source, piece, device):
        k = len(copies)
        held = pack if source is me else out.at[source]
        copy = pltpu.make_async_remote_copy(
            src_ref=held.at[piece], dst_ref=out.at[source, piece], send_sem=send_sem.at[k], recv_sem=recv_sem.at[k],
            device_id=device, device_id_type=MESH,
        )
        copy.start()
        copies[name] = copy

    def arrived(*names):
        for name in names:
            copies[name].wait_recv()

    across = block(z + 2, y_lo, core)
    send("up1", me, first, to_up)
    send("down1", me, second, to_down)
    send("y0a", me, first, to_beside)
    send("y0b", me, second, to_around)
    send("up2", me, second, to_up)
    send("down2", me, first, to_down)
    send("c0", me, whole, to_mate)
    mine = pltpu.make_async_copy(pack, out.at[me], local_sem)
    mine.start()
    arrived("up1")
    send("on_up", down, first, to_up)
    send("y3a", down, first, to_beside)
    arrived("down1")
    send("on_down", up, second, to_down)
    send("y1b", up, second, to_around)
    arrived("up2")
    send("y3b", down, second, to_around)
    arrived("down2")
    send("y1a", up, first, to_beside)
    send("c3", down, whole, to_mate)
    send("c1", up, whole, to_mate)
    arrived("on_up")
    send("y2a", across, first, to_beside)
    arrived("on_down")
    send("y2b", across, second, to_around)
    send("c2", across, whole, to_mate)
    for step in (0, 3, 1, 2):
        arrived("y%da" % step, "y%db" % step)
        send("cy%d" % step, block(z + step, 1 - y_lo, core), whole, to_mate)
    for step in (0, 3, 1, 2):
        arrived("c%d" % step)
    for step in (0, 3, 1, 2):
        arrived("cy%d" % step)
    mine.wait()
    for copy in copies.values():
        copy.wait_send()


def gather_sources(density, pos, nrm, area, n):
    vmem, hbm = pl.BlockSpec(memory_space=pltpu.VMEM), pl.BlockSpec(memory_space=pl.ANY)
    shape = (PACK, pos.shape[1])
    return pl.pallas_call(
        gather_kernel,
        out_shape=jax.ShapeDtypeStruct((n,) + shape, F32),
        in_specs=[vmem] * 4,
        out_specs=hbm,
        scratch_shapes=[
            pltpu.VMEM(shape, F32),
            pltpu.SemaphoreType.DMA((22,)),
            pltpu.SemaphoreType.DMA((22,)),
            pltpu.SemaphoreType.DMA,
        ],
        compiler_params=pltpu.CompilerParams(collective_id=0, has_side_effects=True),
    )(density, pos, nrm, area[None, :])


def reduce_kernel(n, groups, sums, out, first, second, mine, send1, recv1, send2, recv2):
    me, grp = lax.axis_index("blk"), lax.axis_index("grp")
    blk_others = [lax.rem(me + k, n) for k in range(1, n)]
    grp_others = [lax.rem(grp + k, groups) for k in range(1, groups)]
    greet([{"blk": other} for other in blk_others] + [{"grp": other} for other in grp_others])
    copies = []
    for k, other in enumerate(blk_others):
        copy = pltpu.make_async_remote_copy(
            src_ref=sums.at[other], dst_ref=first.at[k], send_sem=send1.at[k], recv_sem=recv1.at[k],
            device_id={"blk": other}, device_id_type=MESH,
        )
        copy.start()
        copies.append(copy)
    total = sums[me]
    for k, copy in enumerate(copies):
        copy.wait_recv()
        total = total + first[k]
    quarters = groups // 2
    for q in range(quarters):
        mine[q] = jnp.concatenate(
            [total[c * quarters + q : c * quarters + q + 1] for c in range(3)] + [jnp.zeros((5, LANES), F32)], axis=0
        )
    more = []
    for k, other in enumerate(grp_others):
        copy = pltpu.make_async_remote_copy(
            src_ref=mine.at[other // 2], dst_ref=second.at[k], send_sem=send2.at[k], recv_sem=recv2.at[k],
            device_id={"grp": other}, device_id_type=MESH,
        )
        copy.start()
        more.append(copy)
    result = mine[grp // 2]
    for k, copy in enumerate(more):
        copy.wait_recv()
        result = result + second[k]
    half = LANES // 2
    out[...] = jnp.where(lax.rem(grp, 2) == 1, result[0:3, half:], result[0:3, 0:half])
    for copy in copies + more:
        copy.wait_send()


def reduce_sources(sums, n, groups):
    vmem = pl.BlockSpec(memory_space=pltpu.VMEM)
    return pl.pallas_call(
        functools.partial(reduce_kernel, n, groups),
        out_shape=jax.ShapeDtypeStruct((3, LANES // 2), F32),
        in_specs=[vmem],
        out_specs=vmem,
        scratch_shapes=[
            pltpu.VMEM((n - 1, SUM_ROWS, LANES), F32),
            pltpu.VMEM((groups - 1, 8, LANES), F32),
            pltpu.VMEM((groups // 2, 8, LANES), F32),
            pltpu.SemaphoreType.DMA((n - 1,)),
            pltpu.SemaphoreType.DMA((n - 1,)),
            pltpu.SemaphoreType.DMA((groups - 1,)),
            pltpu.SemaphoreType.DMA((groups - 1,)),
        ],
        compiler_params=pltpu.CompilerParams(collective_id=1, has_side_effects=True),
    )(sums)


def per_device(
    tgt_pos, tgt_area, tgt_cond, adjoint, src_pos, src_nrm, src_area, density, cond_scale, near_tgt, near_src, near_coef
):
    n, groups = lax.axis_size("blk"), lax.axis_size("grp")
    packs = gather_sources(density, src_pos, src_nrm, src_area, n)
    tgt_grad, sums = pair_sums(
        tgt_pos, tgt_area, tgt_cond, adjoint, cond_scale, near_tgt, near_src, near_coef, packs
    )
    return tgt_grad, reduce_sources(sums, n, groups)


def solution(mesh):
    placed = (
        P(None, ("blk", "grp")),
        P(("blk", "grp")),
        P(("blk", "grp")),
        P(None, ("blk", "grp")),
        P(None, "blk"),
        P(None, "blk"),
        P("blk"),
        P(None, "blk"),
        P(),
        P(("blk", "grp")),
        P(("blk", "grp")),
        P(("blk", "grp")),
    )
    return jax.shard_map(
        per_device,
        mesh=mesh,
        in_specs=placed,
        out_specs=(P(None, ("blk", "grp")), P(None, ("blk", "grp"))),
        check_vma=False,
    )
```

```python
import functools
import math

import jax
import jax.numpy as jnp
from jax import lax
from jax.experimental import pallas as pl
from jax.experimental.pallas import tpu as pltpu
from jax.sharding import PartitionSpec as P

SOFTEN = 0.05
INV_FOUR_PI = 1.0 / (4.0 * math.pi)
MESH = pl.DeviceIdType.MESH
F32 = jnp.float32
BF16 = jnp.bfloat16
LANES = 128
WIDTH = 64
PACK = 72
BLOCK = 256
CHUNK = 512
PIECE = 32
GROUP = 64
SUM_ROWS = 16


def part(x):
    return x.astype(BF16).astype(F32)


def three_parts(x):
    first = part(x)
    second = part(x - first)
    return first, second, part(x - first - second)


def grid_parts(x):
    first = jnp.floor(x * 16.0 + 0.5) * 0.0625
    rest = x - first
    second = part(rest)
    return first, second, part(rest - second), rest


def square_parts(first, rest):
    square = jnp.sum(first * first, axis=0, keepdims=True)
    whole = jnp.floor(square)
    left = jnp.sum((2.0 * first + rest) * rest, axis=0, keepdims=True)
    return whole, square - whole, left


def rows(pieces, total):
    count = sum(p.shape[0] for p in pieces)
    width = pieces[0].shape[1]
    if count < total:
        pieces = list(pieces) + [jnp.zeros((total - count, width), F32)]
    return jnp.concatenate(pieces, axis=0)


def target_features(pos):
    t1, t2, t3, rest = grid_parts(pos)
    whole, fraction, left = square_parts(t1, rest)
    ones = jnp.ones((5, pos.shape[1]), F32)
    return rows([ones, t1, whole, fraction, t1, t1, t2, t2, t2, t3, t3, *three_parts(left)], WIDTH)


def source_features(pos, nrm):
    s1, s2, s3, rest = grid_parts(pos)
    whole, fraction, left = square_parts(s1, rest)
    zero = jnp.zeros((1, pos.shape[1]), F32)
    one = jnp.ones((1, pos.shape[1]), F32)
    radius = rows(
        [whole, fraction, *three_parts(left + SOFTEN)]
        + [-2.0 * s1, one, one, -2.0 * s2, -2.0 * s3, -2.0 * s1, -2.0 * s2, -2.0 * s3, -2.0 * s1, -2.0 * s2]
        + [one, one, one],
        WIDTH,
    )
    triple = 3.0 * nrm
    n1, n2, n3 = three_parts(triple)
    offset = -jnp.sum(triple * pos, axis=0, keepdims=True)
    normal = rows(
        [*three_parts(offset), zero, zero]
        + [n1, zero, zero, n2, n3, n1, n2, n3, n1, n2]
        + [zero, zero, zero],
        WIDTH,
    )
    return radius, normal


def prepare_targets(start, stop, tgt_pos, tgt_area, tgt_cond, adjoint, cond_scale, held, left_m):
    scales = jnp.concatenate([cond_scale[...], jnp.zeros((1, LANES - WIDTH), F32)], axis=1)
    scales = jnp.transpose(jnp.broadcast_to(scales, (LANES, LANES)))[0:WIDTH]
    scales = jnp.concatenate([scales] * (CHUNK // LANES), axis=1)

    def target_prep(i, _):
        cols = pl.ds(pl.multiple_of(i * CHUNK, CHUNK), CHUNK)
        hit = lax.broadcasted_iota(jnp.int32, (WIDTH, CHUNK), 0) == tgt_cond[:, cols]
        weight = tgt_area[:, cols] * jnp.sum(jnp.where(hit, scales, 0.0), axis=0, keepdims=True)
        stacked = jnp.concatenate([adjoint[:, cols] * weight, target_features(tgt_pos[:, cols])], axis=0)
        flat = jnp.transpose(stacked)
        held[cols, :] = flat
        high = part(flat)
        low = flat - high
        lane = lax.broadcasted_iota(jnp.int32, (CHUNK, LANES), 1)
        second = jnp.where(lane >= WIDTH, pltpu.roll(high, WIDTH, 1), low)
        left_m[cols, 0:LANES] = high.astype(BF16)
        left_m[cols, LANES : 2 * LANES] = second.astype(BF16)
        return 0

    lax.fori_loop(start, stop, target_prep, 0)


def pair_kernel(*refs):
    pieces = CHUNK // PIECE
    units = [pltpu.ACC(unit)((PIECE, BLOCK), F32) for unit in range(2) for _ in range(pieces + pieces // 2)]
    pl.run_scoped(lambda *accs: pair_body(accs, *refs), *units)


def pair_body(
    accs,
    near_tgt_in, near_src_in, near_tgt_row, near_src_row, near_coef, held_in, left_in, packs_in,
    tgt_out, src_out,
    held, left_m, packs, near_tgt, near_src, sems, right_m, src_rows, src_table, spread, tgt_sum, src_sum, product, buf0, buf1,
):
    fetches = [
        pltpu.make_async_copy(source, here, sems.at[q])
        for q, (source, here) in enumerate(
            ((packs_in, packs), (left_in, left_m), (held_in, held), (near_tgt_in, near_tgt), (near_src_in, near_src))
        )
    ]
    for fetch in fetches:
        fetch.start()
    tgt_count = held.shape[0]
    parts, _, per = packs.shape
    total = parts * per
    halves = per // BLOCK
    blocks = total // BLOCK
    chunks = tgt_count // CHUNK
    pairs = near_coef.shape[1]

    count = CHUNK // PIECE
    half = count // 2
    radius_acc, first_acc = accs[0:count], accs[count : count + half]
    coupling_acc, second_acc = accs[count + half : 2 * count + half], accs[2 * count + half :]

    zeros = jnp.zeros((WIDTH, BLOCK), BF16)

    def source_prep(b, _):
        for h in range(halves):
            pack = packs[b, :, h * BLOCK : (h + 1) * BLOCK]
            block = b * halves + h
            density = pack[0:WIDTH]
            pos = pack[WIDTH : WIDTH + 3]
            nrm = pack[WIDTH + 3 : WIDTH + 6]
            scaled = density * (pack[WIDTH + 6 : WIDTH + 7] * INV_FOUR_PI)
            high = scaled.astype(BF16)
            low = (scaled - high.astype(F32)).astype(BF16)
            radius, normal = source_features(pos, nrm)
            for q, quarters in enumerate((
                (high, zeros, high, low),
                (zeros, radius.astype(BF16), zeros, zeros),
                (zeros, normal.astype(BF16), zeros, zeros),
            )):
                for r, quarter in enumerate(quarters):
                    right_m[block, q, r * WIDTH : (r + 1) * WIDTH, :] = quarter
            src_rows[block] = pack[WIDTH : WIDTH + 8]
            src_sum[block] = jnp.zeros(src_sum.shape[1:], F32)
            stacked = jnp.concatenate([density, rows([nrm], WIDTH)], axis=0)
            src_table[pl.ds(pl.multiple_of(block * BLOCK, BLOCK), BLOCK), :] = jnp.transpose(stacked)
        return 0

    fetches[0].wait()
    lax.fori_loop(0, parts, source_prep, 0)
    fetches[1].wait()

    feature = lax.broadcasted_iota(jnp.int32, (BLOCK, BLOCK), 0) - WIDTH
    which = lax.broadcasted_iota(jnp.int32, (BLOCK, BLOCK), 1) // LANES
    for unit in range(2):
        axis = which + 2 * unit
        pick = (feature == 5 + axis) | (feature == 16 + axis) | (feature == 25 + axis)
        pltpu.matmul_push_rhs((pick & (axis < 3)).astype(F32).astype(BF16), 0, unit)
    pltpu.matmul_acc_lhs(radius_acc[0], left_m[0:PIECE, :], load_staged_rhs=0)
    pltpu.matmul_acc_lhs(coupling_acc[0], left_m[0:PIECE, :], load_staged_rhs=0)
    pltpu.matmul_pop(radius_acc[0])
    pltpu.matmul_pop(coupling_acc[0])

    def spread_prep(i, _):
        for p in range(count):
            left = left_m[pl.ds(pl.multiple_of(i * CHUNK + p * PIECE, PIECE), PIECE), :]
            pltpu.matmul_acc_lhs(radius_acc[p], left)
            pltpu.matmul_acc_lhs(coupling_acc[p], left)
        for p in range(count):
            at = pl.ds(pl.multiple_of(i * CHUNK + p * PIECE, PIECE), PIECE)
            spread[at, 0 : 2 * LANES] = pltpu.matmul_pop(radius_acc[p])
            spread[at, 2 * LANES :] = pltpu.matmul_pop(coupling_acc[p])[:, 0:LANES]
            tgt_sum[at, :] = jnp.zeros((PIECE, 3 * LANES), F32)
        return 0

    lax.fori_loop(0, chunks, spread_prep, 0)

    for fetch in fetches[2:]:
        fetch.wait()
    first_target = (near_tgt[0] // tgt_count) * tgt_count

    steps = blocks * chunks

    def where(k):
        k = jnp.minimum(k, steps - 1)
        return k // chunks, lax.rem(k, chunks)

    def turn(e, unit, odd):
        if unit == 0:
            whole = [(1, p, radius_acc[p]) for p in range(count)]
            part_of = [(2, p, first_acc[p]) for p in range(half)]
        else:
            whole = [(0, p, coupling_acc[p]) for p in range(count)]
            part_of = [(2, p + half, second_acc[p]) for p in range(half)]
        order = whole + part_of if unit == odd else part_of + whole
        change = len(whole) if unit == odd else len(part_of)
        return order[e] + (e == change or (e == 0 and odd == 0),)

    def enter(e, k, unit, odd):
        b, i = where(k)
        matrix, p, acc, first = turn(e, unit, odd)
        staged = 1 if matrix == 2 else 0
        if first:
            pltpu.matmul_push_rhs(right_m[b, matrix], staged, unit)
        left = left_m[pl.ds(pl.multiple_of(i * CHUNK + p * PIECE, PIECE), PIECE), :]
        pltpu.matmul_acc_lhs(acc, left, load_staged_rhs=staged if first else None)

    def leave(e, buf, unit, odd):
        matrix, p, acc, _ = turn(e, unit, odd)
        buf[p * PIECE : (p + 1) * PIECE, matrix * BLOCK : (matrix + 1) * BLOCK] = pltpu.matmul_pop(acc)

    events = count + half
    per_step = pairs // steps

    def pick_pair(p):
        t = near_tgt[p] - first_target
        product[pl.ds(p, 1), :] = held[pl.ds(t, 1), :] * src_table[pl.ds(near_src[p], 1), :]

    def sums(k, buf, after, odd):
        b, i = where(k)
        base = i * CHUNK
        src = src_rows[b]
        wide = BLOCK // LANES
        lane = [slice(j * LANES, (j + 1) * LANES) for j in range(wide)]
        row = [[jnp.broadcast_to(src[q : q + 1, lane[j]], (8, LANES)) for q in range(6)] for j in range(wide)]
        groups = CHUNK // 8
        acc = None
        for r in range(groups):
            for unit in range(2):
                for e in range(events):
                    if (2 * e + unit) * groups // (2 * events) == r:
                        leave(e, after, unit, odd)
                        enter(e, k + 2, unit, odd)
            for u in range(per_step):
                if u * groups // per_step == r:
                    pick_pair(k * per_step + u)
            if r % GROUP == 0:
                acc = [[None] * 3 for _ in range(wide)]
            at = pl.ds(pl.multiple_of(base + 8 * r, 8), 8)
            here = [spread[at, c * LANES : (c + 1) * LANES] for c in range(3)]
            total_t = [None] * 3
            for j in range(wide):
                cols = slice(8 * r, 8 * r + 8)
                coupling = buf[cols, j * LANES : (j + 1) * LANES]
                radius = buf[cols, BLOCK + j * LANES : BLOCK + (j + 1) * LANES]
                normal = buf[cols, 2 * BLOCK + j * LANES : 2 * BLOCK + (j + 1) * LANES]
                inv = lax.rsqrt(radius)
                inv2 = inv * inv
                scale = (coupling * inv) * inv2
                along = normal * inv2
                for c in range(3):
                    g = scale * (row[j][3 + c] - along * (here[c] - row[j][c]))
                    acc[j][c] = g if acc[j][c] is None else acc[j][c] + g
                    total_t[c] = g if total_t[c] is None else total_t[c] + g
            for c in range(3):
                tgt_sum[at, c * LANES : (c + 1) * LANES] += total_t[c]
            if r % GROUP == GROUP - 1:
                for j in range(wide):
                    for c in range(3):
                        src_sum[b, r // GROUP, 8 * c : 8 * c + 8, lane[j]] += acc[j][c]

    for unit in range(2):
        for e in range(events):
            enter(e, 0, unit, 0)
    for unit in range(2):
        for e in range(events):
            leave(e, buf0, unit, 1)
            enter(e, 1, unit, 1)

    once = jnp.where(near_src[0] >= 0, 1, 0)

    def far(h, _):
        lax.fori_loop(0, once, lambda z, c: (sums(2 * h, buf0, buf1, 0), c)[1], 0)
        lax.fori_loop(0, once, lambda z, c: (sums(2 * h + 1, buf1, buf0, 1), c)[1], 0)
        return 0

    lax.fori_loop(0, steps // 2, far, 0)
    for unit in range(2):
        for e in range(events):
            leave(e, buf0, unit, 0)

    flat = jnp.transpose(product[...])
    coupled = jnp.sum(flat[0:WIDTH], axis=0, keepdims=True) * near_coef[...]
    value = coupled * flat[WIDTH : WIDTH + 3]
    high = part(value)
    both = rows([high, part(value - high)], 8)

    def scatter(index, unit, acc):
        row_at, lane_at = index // BLOCK, lax.rem(index, BLOCK)
        picked = [jnp.where(row_at == g, both, 0.0) for g in range(4 * len(acc))]
        picked = jnp.concatenate(picked, axis=0).astype(BF16)
        lanes = (lax.broadcasted_iota(jnp.int32, (BLOCK, pairs), 0) == lane_at).astype(F32).astype(BF16)
        for q in range(pairs // BLOCK):
            at = slice(q * BLOCK, (q + 1) * BLOCK)
            pltpu.matmul_push_rhs(lanes[:, at], q % 2, unit, transpose=True)
            for p in range(len(acc)):
                load = q % 2 if p == 0 else None
                pltpu.matmul_acc_lhs(acc[p], picked[p * PIECE : (p + 1) * PIECE, at], load_staged_rhs=load)
        return jnp.concatenate([pltpu.matmul_pop(one) for one in acc], axis=0)

    local = near_tgt_row[...] - first_target
    to_tgt = scatter(local, 0, radius_acc[0 : tgt_count // BLOCK // 4])
    to_src = scatter(near_src_row[...], 1, coupling_acc[0 : total // BLOCK // 4])
    wide = BLOCK // LANES

    def near_of(sums_by_row, g):
        near = sums_by_row[8 * (g // wide) : 8 * (g // wide) + 8, g % wide * LANES : (g % wide + 1) * LANES]
        return near[0:3] + near[3:6]

    lane = lax.broadcasted_iota(jnp.int32, (LANES, LANES), 1)
    for g in range(tgt_count // LANES):
        at = slice(g * LANES, (g + 1) * LANES)
        merged = jnp.zeros((LANES, LANES), F32)
        for c in range(3):
            one = jnp.sum(tgt_sum[at, c * LANES : (c + 1) * LANES], axis=1, keepdims=True)
            merged = jnp.where(lane == c, one, merged)
        tgt_out[:, at] = jnp.transpose(merged)[0:3] + near_of(to_tgt, g)
    quarters = per // LANES
    for b in range(parts):
        src_out[b, 3 * quarters :, :] = jnp.zeros((src_out.shape[1] - 3 * quarters, LANES), F32)
        for q in range(quarters):
            g = b * quarters + q
            block, j = divmod(g, BLOCK // LANES)
            near = near_of(to_src, g)
            at = slice(j * LANES, (j + 1) * LANES)
            together = sum(src_sum[block, s, :, at] for s in range(src_sum.shape[1]))
            for c in range(3):
                far_sum = jnp.sum(together[8 * c : 8 * c + 8], axis=0, keepdims=True)
                row = c * quarters + q
                src_out[b, row : row + 1, :] = -far_sum - near[c : c + 1]


def pair_sums(held, left_m, near_tgt, near_src, near_coef, packs):
    tgt_count = held.shape[0]
    pairs = near_coef.shape[0]
    parts, _, per = packs.shape
    total = parts * per
    blocks = total // BLOCK
    vmem, hbm = pl.BlockSpec(memory_space=pltpu.VMEM), pl.BlockSpec(memory_space=pl.ANY)
    return pl.pallas_call(
        pair_kernel,
        out_shape=[
            jax.ShapeDtypeStruct((3, tgt_count), F32),
            jax.ShapeDtypeStruct((parts, SUM_ROWS, LANES), F32),
        ],
        in_specs=[hbm, hbm] + [vmem] * 3 + [hbm] * 3,
        out_specs=[vmem, vmem],
        scratch_shapes=[
            pltpu.VMEM(held.shape, F32),
            pltpu.VMEM(left_m.shape, BF16),
            pltpu.VMEM(packs.shape, F32),
            pltpu.SMEM((pairs,), jnp.int32),
            pltpu.SMEM((pairs,), jnp.int32),
            pltpu.SemaphoreType.DMA((5,)),
            pltpu.VMEM((blocks, 3, BLOCK, BLOCK), BF16),
            pltpu.VMEM((blocks, 8, BLOCK), F32),
            pltpu.VMEM((total, LANES), F32),
            pltpu.VMEM((tgt_count, 3 * LANES), F32),
            pltpu.VMEM((tgt_count, 3 * LANES), F32),
            pltpu.VMEM((blocks, CHUNK // 8 // GROUP, 24, BLOCK), F32),
            pltpu.VMEM((pairs, LANES), F32),
            pltpu.VMEM((CHUNK, 3 * BLOCK), F32),
            pltpu.VMEM((CHUNK, 3 * BLOCK), F32),
        ],
        compiler_params=pltpu.CompilerParams(vmem_limit_bytes=60 * 2**20),
    )(
        near_tgt, near_src, near_tgt[None, :], near_src[None, :], near_coef[None, :], held, left_m, packs,
    )


def greet(peers):
    barrier = pltpu.get_barrier_semaphore()
    for peer in peers:
        pl.semaphore_signal(barrier, inc=1, device_id=peer, device_id_type=MESH)
    pl.semaphore_wait(barrier, len(peers))


def gather_kernel(
    density, pos, nrm, area, tgt_pos_in, tgt_area, tgt_cond, adjoint_in, cond_scale,
    out, held_out, left_out,
    pack, tgt_pos, adjoint, held, left_m, send_sem, recv_sem, local_sem,
):
    reads = [
        pltpu.make_async_copy(tgt_pos_in, tgt_pos, local_sem.at[1]),
        pltpu.make_async_copy(adjoint_in, adjoint, local_sem.at[2]),
    ]
    for read in reads:
        read.start()
    me, grp = lax.axis_index("blk"), lax.axis_index("grp")
    z, y_lo, core = me // 4, lax.rem(me // 2, 2), lax.rem(me, 2)

    def block(z_at, y_at, core_at):
        return (lax.rem(z_at, 4) * 2 + y_at) * 2 + core_at

    up, down = block(z + 1, y_lo, core), block(z + 3, y_lo, core)
    beside, mate = block(z, 1 - y_lo, core), block(z, y_lo, 1 - core)
    other = grp + 1 - 2 * lax.rem(grp, 2)
    to_up, to_down, to_mate = {"blk": up}, {"blk": down}, {"blk": mate}
    to_beside, to_around = {"blk": beside}, {"blk": beside, "grp": other}

    width = density.shape[0]
    pack[0:width, :] = density[...]
    pack[width:, :] = jnp.concatenate(
        [pos[...], nrm[...], area[...], jnp.zeros((PACK - width - 7, pos.shape[1]), F32)], axis=0
    )
    greet([to_up, to_down, to_mate, to_beside, to_around])

    whole, first, second = pl.ds(0, PACK), pl.ds(0, 40), pl.ds(40, PACK - 40)
    copies = {}

    def send(name, source, piece, device):
        k = len(copies)
        held = pack if source is me else out.at[source]
        copy = pltpu.make_async_remote_copy(
            src_ref=held.at[piece], dst_ref=out.at[source, piece], send_sem=send_sem.at[k], recv_sem=recv_sem.at[k],
            device_id=device, device_id_type=MESH,
        )
        copy.start()
        copies[name] = copy

    def arrived(*names):
        for name in names:
            copies[name].wait_recv()

    across = block(z + 2, y_lo, core)
    send("up1", me, first, to_up)
    send("down1", me, second, to_down)
    send("y0a", me, first, to_beside)
    send("y0b", me, second, to_around)
    send("up2", me, second, to_up)
    send("down2", me, first, to_down)
    send("c0", me, whole, to_mate)
    mine = pltpu.make_async_copy(pack, out.at[me], local_sem.at[0])
    mine.start()

    writes = []
    turns = tgt_pos.shape[1] // CHUNK
    stops = [turns * q // 4 for q in range(5)]

    def prepare(q):
        if q == 0:
            for read in reads:
                read.wait()
        prepare_targets(stops[q], stops[q + 1], tgt_pos, tgt_area, tgt_cond, adjoint, cond_scale, held, left_m)
        at = pl.ds(stops[q] * CHUNK, (stops[q + 1] - stops[q]) * CHUNK)
        for i, (here, there) in enumerate(((held, held_out), (left_m, left_out))):
            write = pltpu.make_async_copy(here.at[at], there.at[at], local_sem.at[3 + 2 * q + i])
            write.start()
            writes.append(write)

    prepare(0)
    arrived("up1")
    send("on_up", down, first, to_up)
    send("y3a", down, first, to_beside)
    arrived("down1")
    send("on_down", up, second, to_down)
    send("y1b", up, second, to_around)
    arrived("up2")
    send("y3b", down, second, to_around)
    arrived("down2")
    send("y1a", up, first, to_beside)
    send("c3", down, whole, to_mate)
    send("c1", up, whole, to_mate)
    prepare(1)
    arrived("on_up")
    send("y2a", across, first, to_beside)
    arrived("on_down")
    send("y2b", across, second, to_around)
    send("c2", across, whole, to_mate)
    prepare(2)
    for step in (0, 3, 1, 2):
        arrived("y%da" % step, "y%db" % step)
        send("cy%d" % step, block(z + step, 1 - y_lo, core), whole, to_mate)
    prepare(3)
    for step in (0, 3, 1, 2):
        arrived("c%d" % step)
    for step in (0, 3, 1, 2):
        arrived("cy%d" % step)
    mine.wait()
    for write in writes:
        write.wait()
    for copy in copies.values():
        copy.wait_send()


def gather_sources(density, pos, nrm, area, tgt_pos, tgt_area, tgt_cond, adjoint, cond_scale, n):
    vmem, hbm = pl.BlockSpec(memory_space=pltpu.VMEM), pl.BlockSpec(memory_space=pl.ANY)
    shape = (PACK, pos.shape[1])
    tgt_count = tgt_pos.shape[1]
    return pl.pallas_call(
        gather_kernel,
        out_shape=[
            jax.ShapeDtypeStruct((n,) + shape, F32),
            jax.ShapeDtypeStruct((tgt_count, LANES), F32),
            jax.ShapeDtypeStruct((tgt_count, 2 * LANES), BF16),
        ],
        in_specs=[vmem] * 4 + [hbm, vmem, vmem, hbm, vmem],
        out_specs=[hbm] * 3,
        scratch_shapes=[
            pltpu.VMEM(shape, F32),
            pltpu.VMEM(tgt_pos.shape, F32),
            pltpu.VMEM(adjoint.shape, F32),
            pltpu.VMEM((tgt_count, LANES), F32),
            pltpu.VMEM((tgt_count, 2 * LANES), BF16),
            pltpu.SemaphoreType.DMA((22,)),
            pltpu.SemaphoreType.DMA((22,)),
            pltpu.SemaphoreType.DMA((11,)),
        ],
        compiler_params=pltpu.CompilerParams(
            collective_id=0, has_side_effects=True, vmem_limit_bytes=60 * 2**20
        ),
    )(
        density, pos, nrm, area[None, :], tgt_pos, tgt_area[None, :], tgt_cond[None, :], adjoint, cond_scale[None, :],
    )


def reduce_kernel(n, groups, sums, out, first, second, mine, send1, recv1, send2, recv2):
    me, grp = lax.axis_index("blk"), lax.axis_index("grp")
    blk_others = [lax.rem(me + k, n) for k in range(1, n)]
    grp_others = [lax.rem(grp + k, groups) for k in range(1, groups)]
    greet([{"blk": other} for other in blk_others] + [{"grp": other} for other in grp_others])
    copies = []
    for k, other in enumerate(blk_others):
        copy = pltpu.make_async_remote_copy(
            src_ref=sums.at[other], dst_ref=first.at[k], send_sem=send1.at[k], recv_sem=recv1.at[k],
            device_id={"blk": other}, device_id_type=MESH,
        )
        copy.start()
        copies.append(copy)
    total = sums[me]
    for k, copy in enumerate(copies):
        copy.wait_recv()
        total = total + first[k]
    quarters = groups // 2
    for q in range(quarters):
        mine[q] = jnp.concatenate(
            [total[c * quarters + q : c * quarters + q + 1] for c in range(3)] + [jnp.zeros((5, LANES), F32)], axis=0
        )
    more = []
    for k, other in enumerate(grp_others):
        copy = pltpu.make_async_remote_copy(
            src_ref=mine.at[other // 2], dst_ref=second.at[k], send_sem=send2.at[k], recv_sem=recv2.at[k],
            device_id={"grp": other}, device_id_type=MESH,
        )
        copy.start()
        more.append(copy)
    result = mine[grp // 2]
    for k, copy in enumerate(more):
        copy.wait_recv()
        result = result + second[k]
    half = LANES // 2
    out[...] = jnp.where(lax.rem(grp, 2) == 1, result[0:3, half:], result[0:3, 0:half])
    for copy in copies + more:
        copy.wait_send()


def reduce_sources(sums, n, groups):
    vmem = pl.BlockSpec(memory_space=pltpu.VMEM)
    return pl.pallas_call(
        functools.partial(reduce_kernel, n, groups),
        out_shape=jax.ShapeDtypeStruct((3, LANES // 2), F32),
        in_specs=[vmem],
        out_specs=vmem,
        scratch_shapes=[
            pltpu.VMEM((n - 1, SUM_ROWS, LANES), F32),
            pltpu.VMEM((groups - 1, 8, LANES), F32),
            pltpu.VMEM((groups // 2, 8, LANES), F32),
            pltpu.SemaphoreType.DMA((n - 1,)),
            pltpu.SemaphoreType.DMA((n - 1,)),
            pltpu.SemaphoreType.DMA((groups - 1,)),
            pltpu.SemaphoreType.DMA((groups - 1,)),
        ],
        compiler_params=pltpu.CompilerParams(collective_id=1, has_side_effects=True),
    )(sums)


def per_device(
    tgt_pos, tgt_area, tgt_cond, adjoint, src_pos, src_nrm, src_area, density, cond_scale, near_tgt, near_src, near_coef
):
    n, groups = lax.axis_size("blk"), lax.axis_size("grp")
    packs, held, left_m = gather_sources(
        density, src_pos, src_nrm, src_area, tgt_pos, tgt_area, tgt_cond, adjoint, cond_scale, n
    )
    tgt_grad, sums = pair_sums(held, left_m, near_tgt, near_src, near_coef, packs)
    return tgt_grad, reduce_sources(sums, n, groups)


def solution(mesh):
    placed = (
        P(None, ("blk", "grp")),
        P(("blk", "grp")),
        P(("blk", "grp")),
        P(None, ("blk", "grp")),
        P(None, "blk"),
        P(None, "blk"),
        P("blk"),
        P(None, "blk"),
        P(),
        P(("blk", "grp")),
        P(("blk", "grp")),
        P(("blk", "grp")),
    )
    return jax.shard_map(
        per_device,
        mesh=mesh,
        in_specs=placed,
        out_specs=(P(None, ("blk", "grp")), P(None, ("blk", "grp"))),
        check_vma=False,
    )
```
